256 devices in a mesh: batch: 16 (over z, core), fi: 2 (over x_lo), fj: 8 (over x_hi, y).
Axes of the slice: x: 4 (x_hi: 2, x_lo: 2; x = x_hi * 2 + x_lo), y: 4, z: 8, core: 2. Of those that a mesh axis runs over, the one named last changes fastest.
Arguments:
- student: bfloat16 [8192, 4096], P('batch', 'fi'), may hold values from -500 to 500
- teacher: bfloat16 [8192, 4096], P('batch', ('fi', 'fj')), may hold values from -500 to 500
Outputs:
- student_grad: float32 [8192, 4096], P('batch', ('fi', 'fj'))
The draws below stay inside these ranges and needn't reach their ends.
All inputs are finite; a program needn't handle non-finite values.
Results may differ from the reference program's by a relative error of at most 0.0052.
Values may be sent and summed in bfloat16 or wider, within the bound.
No kernel may reach another device: no remote copies, remote signals or barrier semaphores. Data moves between devices by JAX's collectives and lax.ppermute only.
A program may use at most 128 MiB of HBM per device.

```python
import math
import jax
import jax.numpy as jnp
from jax import lax

F = 4096
TOKENS = 8192


def common_base(key):
    return jax.random.normal(key, (TOKENS, F), jnp.float32)


def features(key, base, mix):
    first, second, third, fourth = jax.random.split(key, 4)
    noise = jax.random.normal(first, (TOKENS, F), jnp.float32)
    row_scale = jnp.exp(jax.random.uniform(second, (TOKENS, 1), jnp.float32, 0.0, math.log(10.0)))
    col_scale = jnp.exp(jax.random.uniform(third, (1, F), jnp.float32, math.log(0.5), math.log(5.0)))
    offset = jax.random.uniform(fourth, (1, F), jnp.float32, -1.0, 1.0)
    value = (mix * base + 0.7 * noise) * row_scale * col_scale + offset
    return value.astype(jnp.bfloat16)


def draw_student(key, part):
    base = common_base(key)
    key = jax.random.fold_in(key, 1)
    return features(key, base, 0.7)


def draw_teacher(key, part):
    base = common_base(key)
    key = jax.random.fold_in(key, 2)
    return features(key, base, 0.6)


def setup_inputs(seed: int = 0) -> dict:
    seeds = jax.random.split(jax.random.key(seed), 3)
    return {
        "student": draw_student(jax.random.fold_in(seeds[2], 71), 0),
        "teacher": draw_teacher(jax.random.fold_in(seeds[2], 71), 0),
    }


EPSILON = 1e-05
OFF_CROSS = 0.5
OFF_AUTO = 0.25

def standardize(values, total, square_total, clip_total):
    center = total / clip_total
    spread = square_total / clip_total - center * center
    scale = lax.rsqrt(spread + EPSILON)
    return ((values - center) * scale, scale)

def reference(student, teacher):
    clip_total = student.shape[0]
    student_wide = student.astype(jnp.float32)
    teacher_wide = teacher.astype(jnp.float32)
    scaled_student, student_scale = standardize(student_wide, lax.optimization_barrier(jnp.sum(student_wide, 0)), lax.optimization_barrier(jnp.sum(student_wide * student_wide, 0)), clip_total)
    scaled_teacher = standardize(teacher_wide, lax.optimization_barrier(jnp.sum(teacher_wide, 0)), lax.optimization_barrier(jnp.sum(teacher_wide * teacher_wide, 0)), clip_total)[0]
    student_half = scaled_student.astype(jnp.bfloat16)
    teacher_half = scaled_teacher.astype(jnp.bfloat16)
    cross = jnp.dot(student_half.T, teacher_half, preferred_element_type=jnp.float32) / clip_total
    auto = jnp.dot(student_half.T, student_half, preferred_element_type=jnp.float32) / clip_total
    on_diagonal = jnp.eye(F, dtype=bool)
    grad_cross = jnp.where(on_diagonal, 2.0 * (cross - 1.0), 2.0 * OFF_CROSS * cross).astype(jnp.bfloat16)
    grad_auto = jnp.where(on_diagonal, 0.0, 2.0 * OFF_AUTO * auto).astype(jnp.bfloat16)
    direct = jnp.dot(teacher_half, grad_cross.T, preferred_element_type=jnp.float32) + jnp.dot(student_half, (grad_auto * 2).T, preferred_element_type=jnp.float32)
    mean_direct = lax.optimization_barrier(jnp.sum(direct, 0)) / clip_total
    mean_product = lax.optimization_barrier(jnp.sum(direct * scaled_student, 0)) / clip_total
    return student_scale * (direct - mean_direct - scaled_student * mean_product)
```

```python
import functools

import jax
import jax.numpy as jnp
from jax import lax
from jax.experimental import pallas as pl
from jax.experimental.pallas import tpu as pltpu
from jax.sharding import PartitionSpec as P

EPSILON = 1e-05
BF = jnp.bfloat16
F32 = jnp.float32
NZ, NC, NX, NY = 8, 2, 4, 4
BLK = 256
PAD = 16
VMEM = 40 * 1024 * 1024
PARAMS = pltpu.CompilerParams(vmem_limit_bytes=VMEM)


def z_shift(value, step):
    return lax.ppermute(
        value,
        "batch",
        [(z * NC + c, ((z + step) % NZ) * NC + c) for z in range(NZ) for c in range(NC)],
    )


def z_swap(value, bit):
    return lax.ppermute(
        value, "batch", [(z * NC + c, (z ^ bit) * NC + c) for z in range(NZ) for c in range(NC)]
    )


def core_swap(value):
    return lax.ppermute(value, "batch", [(b, b ^ 1) for b in range(NZ * NC)])


def y_shift(value, step):
    return lax.ppermute(
        value,
        "fj",
        [(h * NY + y, h * NY + (y + step) % NY) for h in range(2) for y in range(NY)],
    )


def x_flat(x, y):
    return (x % 2) * 8 + (x // 2) * NY + y


def x_move(value, target):
    return lax.ppermute(
        value,
        ("fi", "fj"),
        [(x_flat(x, y), x_flat(target(x) % NX, y)) for x in range(NX) for y in range(NY)],
    )


def x_partner(value):
    return x_move(value, lambda x: x ^ 1)


def x_far(value):
    return x_move(value, lambda x: x - 1 if x % 2 == 0 else x + 1)


def x_opposite(value):
    return x_move(value, lambda x: x + 2)


def dot(a, b, dims):
    return lax.dot_general(a, b, (dims, ((), ())), preferred_element_type=F32)


def first_kernel(z_ref, rows_own, rows_other, keep, other, top, bottom):
    part = dot(rows_own[...], keep[0], ((1,), (0,))) + dot(
        rows_other[...], other[0], ((1,), (0,))
    )
    half = top.shape[0]
    top[...] = part[:half].astype(BF)
    bottom[...] = part[half:].astype(BF)


def rest_kernel(z_ref, rows_own, rows_other, keep, other, out):
    out[0] = dot(rows_own[...], keep[0], ((1,), (0,))) + dot(
        rows_other[...], other[0], ((1,), (0,))
    )


def rest_offset(i):
    return jnp.where(i % 2 == 0, 3 - i // 2, 5 + i // 2)


def first_product(z, rows_own, rows_other, keep, other, half):
    rows, clips = rows_own.shape
    whole = pl.BlockSpec((rows, clips), lambda i, z: (0, 0))
    block = pl.BlockSpec((1, clips, BLK), lambda i, z: ((z[0] + 4) % NZ, 0, 0))
    return pl.pallas_call(
        first_kernel,
        grid_spec=pltpu.PrefetchScalarGridSpec(
            num_scalar_prefetch=1,
            grid=(1,),
            in_specs=[whole, whole, block, block],
            out_specs=[
                pl.BlockSpec((half, BLK), lambda i, z: (0, 0)),
                pl.BlockSpec((rows - half, BLK), lambda i, z: (0, 0)),
            ],
        ),
        out_shape=[
            jax.ShapeDtypeStruct((half, BLK), BF),
            jax.ShapeDtypeStruct((rows - half, BLK), BF),
        ],
        compiler_params=PARAMS,
        name="first_product",
    )(z, rows_own, rows_other, keep, other)


def rest_products(z, rows_own, rows_other, keep, other):
    rows, clips = rows_own.shape
    whole = pl.BlockSpec((rows, clips), lambda i, z: (0, 0))
    block = pl.BlockSpec((1, clips, BLK), lambda i, z: ((z[0] + rest_offset(i)) % NZ, 0, 0))
    return pl.pallas_call(
        rest_kernel,
        grid_spec=pltpu.PrefetchScalarGridSpec(
            num_scalar_prefetch=1,
            grid=(7,),
            in_specs=[whole, whole, block, block],
            out_specs=pl.BlockSpec((1, rows, BLK), lambda i, z: (i, 0, 0)),
        ),
        out_shape=jax.ShapeDtypeStruct((7, rows, BLK), F32),
        compiler_params=PARAMS,
        cost_estimate=pl.CostEstimate(
            flops=7 * 4 * rows * clips * BLK, bytes_accessed=9 << 20, transcendentals=0
        ),
        name="rest_products",
    )(z, rows_own, rows_other, keep, other)


def early_add_kernel(right, left, from_left, from_right, out_right, out_left):
    half = from_left.shape[0]
    out_right[:half] = (right[0, :half] + from_left[...].astype(F32)).astype(BF)
    out_right[half:] = right[0, half:].astype(BF)
    out_left[:half] = left[0, :half].astype(BF)
    out_left[half:] = (left[0, half:] + from_right[...].astype(F32)).astype(BF)


def add_kernel(right, left, from_left, from_right, out_right, out_left):
    out_right[...] = (right[0] + from_left[...].astype(F32)).astype(BF)
    out_left[...] = (left[0] + from_right[...].astype(F32)).astype(BF)


def ring_add(kernel, parts, index, from_left, from_right):
    rows = parts.shape[1]
    part = lambda k: pl.BlockSpec((1, rows, BLK), lambda i: (k, 0, 0))
    plain = lambda a: pl.BlockSpec(a.shape, lambda i: (0, 0))
    return pl.pallas_call(
        kernel,
        grid=(1,),
        in_specs=[part(index), part(index + 1), plain(from_left), plain(from_right)],
        out_specs=[pl.BlockSpec((rows, BLK), lambda i: (0, 0))] * 2,
        out_shape=[jax.ShapeDtypeStruct((rows, BLK), BF)] * 2,
        compiler_params=PARAMS,
        name="ring_add",
    )(parts, parts, from_left, from_right)


def gradient_kernel(clip_total, place, part, from_left, from_right, top, bottom):
    total = part[0] + from_left[...].astype(F32) + from_right[...].astype(F32)
    value = total * (1.0 / clip_total)
    top_value = value[:BLK]
    row = lax.broadcasted_iota(jnp.int32, (BLK, BLK), 0)
    col = lax.broadcasted_iota(jnp.int32, (BLK, BLK), 1)
    owner = jnp.where(place[0] == 0, 1, 0)
    diagonal = jnp.where(row == col, owner, 0) == 1
    on = jnp.where(place[1] == 0, 2.0 * (top_value - 1.0), 0.0)
    top[...] = jnp.where(diagonal, on, top_value).astype(BF)
    bottom[...] = value[BLK:].astype(BF)


def gradient(place, parts, from_left, from_right, clip_total):
    rows = parts.shape[1]
    plain = lambda a: pl.BlockSpec(a.shape, lambda i, p: (0, 0))
    return pl.pallas_call(
        functools.partial(gradient_kernel, clip_total),
        grid_spec=pltpu.PrefetchScalarGridSpec(
            num_scalar_prefetch=1,
            grid=(1,),
            in_specs=[
                pl.BlockSpec((1, rows, BLK), lambda i, p: (6, 0, 0)),
                plain(from_left),
                plain(from_right),
            ],
            out_specs=[
                pl.BlockSpec((BLK, BLK), lambda i, p: (0, 0)),
                pl.BlockSpec((rows - BLK, BLK), lambda i, p: (0, 0)),
            ],
        ),
        out_shape=[
            jax.ShapeDtypeStruct((BLK, BLK), BF),
            jax.ShapeDtypeStruct((rows - BLK, BLK), BF),
        ],
        compiler_params=PARAMS,
        name="gradient",
    )(place, parts, from_left, from_right)


def direct_kernel(offsets, has_acc, out_rows, place, keep, other, *refs):
    count = len(offsets)
    tops, bottoms = refs[:count], refs[count : 2 * count]
    refs = refs[2 * count :]
    if has_acc:
        acc_own, acc_other, acc_sums = refs[:3]
        refs = refs[3:]
    own, away, sums = refs
    clips = keep.shape[1]
    ones = jnp.ones((PAD, BLK), BF)
    z, core = place[0], place[1]
    row = lax.broadcasted_iota(jnp.int32, (BLK, BLK), 0)
    col = lax.broadcasted_iota(jnp.int32, (BLK, BLK), 1)
    for half in range(2):
        lanes = pl.ds(half * BLK, BLK)
        total_own = acc_own[:, lanes] if has_acc else None
        total_away = acc_other[:, lanes] if has_acc else None
        total_sums = acc_sums[:, lanes] if has_acc else None
        for k in range(count):
            index = lax.rem(z + offsets[k] + NZ, NZ)
            grad = tops[k][...] if half == 0 else bottoms[k][:BLK]
            column_sums = bottoms[k][BLK:]
            product = dot(keep[index], grad, ((1,), (1,)))
            total_own = product if total_own is None else total_own + product
            product = dot(other[index], grad, ((1,), (1,)))
            total_away = product if total_away is None else total_away + product
            wide = grad.astype(F32)
            square = wide * wide
            if half == 0:
                owner = jnp.where(index == 0, 1, 0) * jnp.where(core == 0, 1, 0)
                diagonal = jnp.where(row == col, owner, 0) == 1
                square = jnp.where(diagonal, wide * (wide * 0.5 + 1.0), square)
            high = square.astype(BF)
            low = (square - high.astype(F32)).astype(BF)
            product = dot(ones, high, ((1,), (1,))) + dot(ones, low, ((1,), (1,)))
            shift = dot(column_sums, grad, ((1,), (1,)))
            line = lax.broadcasted_iota(jnp.int32, (PAD, BLK), 0)
            both = jnp.where(line == 0, shift, jnp.where(line == 1, product, 0.0))
            total_sums = both if total_sums is None else total_sums + both
        own[:, lanes] = total_own
        away[:, lanes] = total_away
        sums[:, lanes] = total_sums


def direct_part(place, keep, other, offsets, tops, bottoms, acc):
    clips = keep.shape[1]
    width = 2 * BLK
    operands = [keep, other, *tops, *bottoms, *(acc or [])]

    def spec(a):
        return pl.BlockSpec(a.shape, lambda i, p, n=a.ndim: (0,) * n)

    shapes = [(clips, width), (clips, width), (PAD, width)]
    return pl.pallas_call(
        functools.partial(direct_kernel, offsets, acc is not None, clips),
        grid_spec=pltpu.PrefetchScalarGridSpec(
            num_scalar_prefetch=1,
            grid=(1,),
            in_specs=[spec(a) for a in operands],
            out_specs=[pl.BlockSpec(s, lambda i, p: (0, 0)) for s in shapes],
        ),
        out_shape=[jax.ShapeDtypeStruct(s, F32) for s in shapes],
        compiler_params=PARAMS,
        cost_estimate=pl.CostEstimate(
            flops=len(offsets) * 4 * clips * width * BLK,
            bytes_accessed=9 << 20,
            transcendentals=0,
        ),
        name="direct_part",
    )(place, *operands)


def normalize(values, center, scale):
    return ((values.astype(F32) - center) * scale).astype(BF)


def body(student, teacher):
    clips = student.shape[0]
    clip_total = clips * NZ * NC
    batch = lax.axis_index("batch")
    z, core = batch // NC, batch % NC
    fj = lax.axis_index("fj")
    x_hi, y = fj // NY, fj % NY

    def column(hi, step):
        return (hi * NY + (y + step) % NY) * BLK

    def cut(array, start, axis=1):
        return lax.dynamic_slice_in_dim(array, start, BLK, axis)

    with jax.named_scope("operand_blocks"):
        teacher_blocks = [teacher] + [None] * 7
        teacher_blocks[4] = x_partner(teacher)
        for base in (0, 4):
            own = teacher_blocks[base]
            teacher_blocks[base + 1] = y_shift(own, -1)
            teacher_blocks[base + 3] = y_shift(own, 1)
            teacher_blocks[base + 2] = y_shift(own, 2)
        far = jnp.stack([cut(student, column(1 - x_hi, k)) for k in range(3)])
        far = x_far(far)
        near = x_partner(cut(student, column(x_hi, 3)))
        student_blocks = [cut(student, column(x_hi, k)) for k in range(4)]
        student_blocks += [far[0], far[1], far[2], near]
        other_slab = cut(student, column(1 - x_hi, 0))

    with jax.named_scope("statistics"):
        student_wide = student.astype(F32)
        teacher_wide = teacher.astype(F32)
        totals = jnp.concatenate(
            [
                jnp.stack([jnp.sum(student_wide, 0), jnp.sum(student_wide * student_wide, 0)]),
                jnp.stack([jnp.sum(teacher_wide, 0), jnp.sum(teacher_wide * teacher_wide, 0)]),
            ],
            1,
        )
        totals = totals + core_swap(totals)
        for bit in (1, 2, 4):
            totals = totals + z_swap(totals, bit)
        center = totals[0] / clip_total
        scale = lax.rsqrt(totals[1] / clip_total - center * center + EPSILON)
        figures = jnp.stack([center, scale])
        block = student.shape[1]
        partner_figures = x_partner(figures)
        pair = jnp.stack([figures[:, block:], partner_figures[:, block:]])
        turned = [pair, y_shift(pair, -1), y_shift(pair, 2), y_shift(pair, 1)]
        teacher_figures = [turned[k % 4][k // 4] for k in range(8)]
        student_figures = [cut(figures, column(x_hi, k)) for k in range(4)]
        student_figures += [cut(partner_figures, column(x_hi, k)) for k in range(4)]
        other_figures = cut(figures, column(1 - x_hi, 0))

    with jax.named_scope("normalize"):
        teacher_half = jnp.stack(
            [normalize(v, f[0], f[1]) for v, f in zip(teacher_blocks, teacher_figures)]
        )
        student_half = jnp.stack(
            [normalize(v, f[0], f[1]) for v, f in zip(student_blocks, student_figures)]
        )
        keep = jnp.where(core == 0, teacher_half, student_half)
        other = core_swap(jnp.where(core == 0, student_half, teacher_half))
        slabs = jnp.concatenate(
            [
                normalize(student_blocks[0], student_figures[0][0], student_figures[0][1]),
                normalize(other_slab, other_figures[0], other_figures[1]),
            ],
            1,
        )
        extra = (lax.broadcasted_iota(jnp.int32, (PAD, clips), 0) == 0).astype(BF)
        rows_own = jnp.concatenate([slabs.T, extra], 0)
        rows_other = core_swap(rows_own)

    place = jnp.stack([z, core]).astype(jnp.int32)
    with jax.named_scope("reduce"):
        top, bottom = first_product(place, rows_own, rows_other, keep, other, BLK)
        right, left = z_shift(top, 1), z_shift(bottom, -1)
        parts = rest_products(place, rows_own, rows_other, keep, other)
        for step in range(3):
            kernel = early_add_kernel if step == 0 else add_kernel
            right, left = ring_add(kernel, parts, 2 * step, right, left)
            right, left = z_shift(right, 1), z_shift(left, -1)
        top, bottom = gradient(place, parts, right, left, clip_total)

    with jax.named_scope("spread"):
        tops, bottoms = {0: top}, {0: bottom}
        for k in range(1, 5):
            tops[-k] = z_shift(tops[1 - k], 1)
            bottoms[k] = z_shift(bottoms[k - 1], -1)
            if k < 4:
                bottoms[-k] = z_shift(bottoms[1 - k], 1)
                tops[k] = z_shift(tops[k - 1], -1)
        tops[4], bottoms[-4] = tops[-4], bottoms[4]

    with jax.named_scope("direct"):
        acc = None
        for offsets in ((0, -1, 1, -2, 2), (-3, 3, 4)):
            acc = direct_part(
                place,
                keep,
                other,
                offsets,
                [tops[k] for k in offsets],
                [bottoms[k] for k in offsets],
                acc,
            )
        own, away, sums = acc
        wide = jnp.concatenate([own, sums], 0) + core_swap(jnp.concatenate([away, sums], 0))
        sent = wide[:, BLK:]
        high = sent.astype(BF)
        low = (sent[clips:] - high[clips:].astype(F32)).astype(BF)
        arrived = x_opposite(jnp.concatenate([high, low], 0)).astype(F32)
        direct = wide[:clips, :BLK] + arrived[:clips]
        sums = wide[clips:, :BLK] + arrived[clips : clips + PAD] + arrived[clips + PAD :]

    with jax.named_scope("student_grad"):
        own_center, own_scale = student_figures[0]
        own_scaled = (student_blocks[0].astype(F32) - own_center) * own_scale
        return own_scale * (direct - sums[0] - own_scaled * sums[1])


def solution(mesh):
    placed = (P("batch", "fi"), P("batch", ("fi", "fj")))
    return jax.shard_map(
        body, mesh=mesh, in_specs=placed, out_specs=P("batch", ("fi", "fj")), check_vma=False
    )
```

```python
import functools

import jax
import jax.numpy as jnp
from jax import lax
from jax.experimental import pallas as pl
from jax.experimental.pallas import tpu as pltpu
from jax.sharding import PartitionSpec as P

EPSILON = 1e-05
BF = jnp.bfloat16
F32 = jnp.float32
NZ, NC, NX, NY = 8, 2, 4, 4
BLK = 256
PAD = 16
PARAMS = pltpu.CompilerParams(vmem_limit_bytes=28 * 1024 * 1024)


def move(value, target):
    flat = lambda z, c, x, y: (z % NZ * NC + c) * 16 + x % 2 * 8 + x // 2 * NY + y % NY
    pairs = []
    for z in range(NZ):
        for c in range(NC):
            for x in range(NX):
                for y in range(NY):
                    to = target(z, c, x, y)
                    if to is not None:
                        pairs.append((flat(z, c, x, y), flat(*to)))
    return lax.ppermute(value, ("batch", "fi", "fj"), pairs)


def z_shift(value, step):
    return move(value, lambda z, c, x, y: (z + step, c, x, y))


def z_swap(value, bit):
    return move(value, lambda z, c, x, y: (z ^ bit, c, x, y))


def core_swap(value):
    return move(value, lambda z, c, x, y: (z, 1 - c, x, y))


def far(x):
    return (x + 3) % NX if x % 2 == 0 else (x + 1) % NX


def dot(a, b, dims):
    return lax.dot_general(a, b, (dims, ((), ())), preferred_element_type=F32)


def whole(a):
    return pl.BlockSpec(a.shape, lambda i, *p, n=a.ndim: (0,) * n)


def call(kernel, name, scalars, operands, in_specs, shapes, out_specs=None, grid=(1,), flops=0):
    outs = [jax.ShapeDtypeStruct(s, d) for s, d in shapes]
    return pl.pallas_call(
        kernel,
        grid_spec=pltpu.PrefetchScalarGridSpec(
            num_scalar_prefetch=1,
            grid=grid,
            in_specs=[whole(a) if s is None else s for a, s in zip(operands, in_specs)],
            out_specs=out_specs or [whole(o) for o in outs],
        ),
        out_shape=outs,
        compiler_params=PARAMS,
        cost_estimate=pl.CostEstimate(flops=flops, bytes_accessed=1 << 20, transcendentals=0),
        name=name,
    )(scalars, *operands)


def sums_kernel(place, student, teacher, out):
    def add(values):
        values = values.astype(F32)
        return jnp.concatenate(
            [jnp.sum(values, 0, keepdims=True), jnp.sum(values * values, 0, keepdims=True)], 0
        )

    width = student.shape[1]
    for start in range(0, width, 512):
        out[:, start : start + 512] = add(student[:, start : start + 512])
    out[:, width:] = add(teacher[...])


def figures_of(totals, clip_total):
    center = totals[0:1] / clip_total
    scale = lax.rsqrt(totals[1:2] / clip_total - center * center + EPSILON)
    return center, scale


def normalize_kernel(clip_total, place, *refs):
    blocks, slabs = refs[:8], refs[8:10]
    totals, partner, turned = refs[10], refs[11], refs[12:15]
    operand, rows = refs[15:]
    core, x_hi, y = place[1], place[2], place[3]
    half = totals.shape[1] - BLK
    tile = blocks[0].shape[0]

    def student_totals(ref, hi, step):
        column = (hi * NY + lax.rem(y + step, NY)) * BLK
        return ref[:, pl.ds(pl.multiple_of(column, BLK), BLK)]

    def scaled(values, block_totals):
        center, scale = figures_of(block_totals, clip_total)
        return (values.astype(F32) - center) * scale

    for k in range(8):
        source = totals if k < 4 else partner
        if k % 4 == 0:
            teacher_totals = source[:, half:]
        else:
            teacher_totals = turned[k % 4 - 1][k // 4]
        block_totals = jnp.where(core == 0, teacher_totals, student_totals(source, x_hi, k % 4))
        operand[k] = scaled(blocks[k][...], block_totals).astype(BF)
    for k in range(2):
        hi = x_hi if k == 0 else 1 - x_hi
        values = scaled(slabs[k][...], student_totals(totals, hi, 0))
        rows[k * BLK : (k + 1) * BLK] = values.T.astype(BF)
    line = lax.broadcasted_iota(jnp.int32, (PAD, tile), 0)
    rows[2 * BLK :] = jnp.where(line == 0, 1.0, 0.0).astype(BF)


def first_kernel(place, rows, block, top, bottom):
    part = dot(rows[...], block[0], ((1,), (0,)))
    top[...] = part[:BLK].astype(BF)
    bottom[...] = part[BLK:].astype(BF)


def pair_kernel(send, place, rows, ahead, behind, *outs):
    ahead_top, ahead_bottom, behind_top, behind_bottom = outs
    part = dot(rows[...], ahead[0], ((1,), (0,)))
    ahead_top[...] = part[:BLK]
    ahead_bottom[...] = part[BLK:].astype(ahead_bottom.dtype)
    part = dot(rows[...], behind[0], ((1,), (0,)))
    behind_top[...] = part[:BLK].astype(behind_top.dtype)
    behind_bottom[...] = part[BLK:]


def own_kernel(place, rows, block, out):
    out[...] = dot(rows[...], block[0], ((1,), (0,)))


def add_kernel(place, ahead, behind, from_left, from_right, out_right, out_left):
    out_right[...] = (ahead[...] + from_left[...].astype(F32)).astype(BF)
    out_left[...] = (behind[...] + from_right[...].astype(F32)).astype(BF)


def gradient_kernel(clip_total, place, part, top_a, top_b, bottom_a, bottom_b, top, bottom):
    factor = 1.0 / clip_total
    value = (part[:BLK] + top_a[...].astype(F32) + top_b[...].astype(F32)) * factor
    row = lax.broadcasted_iota(jnp.int32, (BLK, BLK), 0)
    col = lax.broadcasted_iota(jnp.int32, (BLK, BLK), 1)
    owner = jnp.where(place[0] == 0, 1, 0)
    diagonal = jnp.where(row == col, owner, 0) == 1
    on = jnp.where(place[1] == 0, 2.0 * (value - 1.0), 0.0)
    top[...] = jnp.where(diagonal, on, value).astype(BF)
    value = (part[BLK:] + bottom_a[...].astype(F32) + bottom_b[...].astype(F32)) * factor
    bottom[...] = value.astype(BF)


def operand_spec(operand, offset):
    return pl.BlockSpec(
        (1, *operand.shape[1:]), lambda i, p: (lax.rem(p[0] + (offset + NZ), NZ), 0, 0)
    )


def reduce_rows(place, rows, operand, clip_total):
    height = rows.shape[0]
    low = height - BLK
    flops = 2 * height * rows.shape[1] * BLK
    top, bottom = call(
        first_kernel,
        "product_far",
        place,
        [rows, operand],
        [None, operand_spec(operand, 4)],
        [((BLK, BLK), BF), ((low, BLK), BF)],
        flops=flops,
    )

    def pair(distance, kind):
        return call(
            functools.partial(pair_kernel, kind == BF),
            "product_pair",
            place,
            [rows, operand, operand],
            [None, operand_spec(operand, distance), operand_spec(operand, -distance)],
            [((BLK, BLK), F32), ((low, BLK), kind), ((BLK, BLK), kind), ((low, BLK), F32)],
            flops=2 * flops,
        )

    def add(ahead, behind, from_left, from_right):
        shapes = [(ahead.shape, BF), (behind.shape, BF)]
        operands = [ahead, behind, from_left, from_right]
        return call(add_kernel, "ring_add", place, operands, [None] * 4, shapes)

    def send(right, left):
        return z_shift(right, 1), z_shift(left, -1)

    a = send(top, bottom)
    at, ab, bt, bb = pair(3, BF)
    b = send(ab, bt)
    a = send(*add(at, bb, *a))
    at, ab, bt, bb = pair(2, F32)
    b = send(*add(ab, bt, *b))
    a = send(*add(at, bb, *a))
    at, ab, bt, bb = pair(1, F32)
    b = send(*add(ab, bt, *b))
    a = send(*add(at, bb, *a))
    (own,) = call(
        own_kernel,
        "product_own",
        place,
        [rows, operand],
        [None, operand_spec(operand, 0)],
        [((height, BLK), F32)],
        flops=flops,
    )
    return call(
        functools.partial(gradient_kernel, clip_total),
        "gradient",
        place,
        [own, a[0], b[1], b[0], a[1]],
        [None] * 5,
        [((BLK, BLK), BF), ((low, BLK), BF)],
    )


def direct_kernel(offsets, has_acc, last, place, *refs):
    count = len(offsets)
    blocks, tops, bottoms = refs[:count], refs[count : 2 * count], refs[2 * count : 3 * count]
    acc = refs[3 * count] if has_acc else None
    outs = refs[3 * count + (1 if has_acc else 0) :]
    clips = blocks[0].shape[1]
    ones = jnp.ones((PAD, BLK), BF)
    z, core = place[0], place[1]
    row = lax.broadcasted_iota(jnp.int32, (BLK, BLK), 0)
    col = lax.broadcasted_iota(jnp.int32, (BLK, BLK), 1)
    line = lax.broadcasted_iota(jnp.int32, (PAD, BLK), 0)
    for half in (1, 0):
        lanes = slice(half * BLK, half * BLK + BLK)
        total = acc[:clips, lanes] if has_acc else None
        sums = acc[clips:, lanes] if has_acc else None
        for k in range(count):
            grad = tops[k][...] if half == 0 else bottoms[k][:BLK]
            product = dot(blocks[k][0], grad, ((1,), (1,)))
            total = product if total is None else total + product
            wide = grad.astype(F32)
            square = wide * wide
            if half == 0:
                index = lax.rem(z + (offsets[k] + NZ), NZ)
                owner = jnp.where(index == 0, 1, 0) * jnp.where(core == 0, 1, 0)
                diagonal = jnp.where(row == col, owner, 0) == 1
                square = jnp.where(diagonal, wide * (wide * 0.5 + 1.0), square)
            high = square.astype(BF)
            low = (square - high.astype(F32)).astype(BF)
            product = dot(ones, high, ((1,), (1,))) + dot(ones, low, ((1,), (1,)))
            shift = dot(bottoms[k][BLK:], grad, ((1,), (1,)))
            both = jnp.where(line == 0, shift, jnp.where(line == 1, product, 0.0))
            sums = both if sums is None else sums + both
        if last:
            middle = clips // 2
            for part in range(2):
                out = outs[2 * half + part]
                out[:middle] = total[part * middle : part * middle + middle]
                out[middle:] = sums
        else:
            outs[0][:clips, lanes] = total
            outs[0][clips:, lanes] = sums


def direct_part(place, operand, offsets, tops, bottoms, acc, last):
    clips = operand.shape[1]
    operands = [operand] * len(offsets)
    specs = [operand_spec(operand, k) for k in offsets]
    more = [tops[k] for k in offsets] + [bottoms[k] for k in offsets]
    more += [] if acc is None else [acc]
    if last:
        shapes = [((clips // 2 + PAD, BLK), F32)] * 4
    else:
        shapes = [((clips + PAD, 2 * BLK), F32)]
    return call(
        functools.partial(direct_kernel, offsets, acc is not None, last),
        "direct_part",
        place,
        operands + more,
        specs + [None] * len(more),
        shapes,
        flops=len(offsets) * 4 * clips * BLK * BLK,
    )


def body(student, teacher):
    clips = student.shape[0]
    clip_total = clips * NZ * NC
    batch = lax.axis_index("batch")
    z, core = batch // NC, batch % NC
    fj = lax.axis_index("fj")
    x_hi, y = fj // NY, fj % NY
    place = jnp.stack([z, core, x_hi, y]).astype(jnp.int32)
    cross = core == 0

    def cut(hi, step):
        column = (hi * NY + (y + step) % NY) * BLK
        return lax.dynamic_slice_in_dim(student, column, BLK, 1)

    def join(mine, others):
        return jnp.concatenate([mine, others], 0)

    with jax.named_scope("statistics"):
        (totals,) = call(
            sums_kernel,
            "column_sums",
            place,
            [student, teacher],
            [None] * 2,
            [((2, student.shape[1] + BLK), F32)],
        )
        totals = totals + core_swap(totals)
        for bit in (1, 2, 4):
            totals = totals + z_swap(totals, bit)
        partner = move(totals, lambda z, c, x, y: (z, c, x ^ 1, y))
        half = student.shape[1]
        pair = jnp.stack([totals[:, half:], partner[:, half:]])
        turned = [move(pair, lambda z, c, x, y, k=k: (z, c, x, y - k)) for k in (1, 2, 3)]

    with jax.named_scope("operand_blocks"):
        mine = [cut(x_hi, k) for k in range(4)]
        away = [cut(1 - x_hi, k) for k in range(3)]
        second = jnp.where(cross, away[1], teacher)
        third = jnp.where(cross, away[2], mine[0])
        early = core_swap(jnp.stack([away[0], second, third, mine[3]]))
        late = core_swap(jnp.stack(mine[:3]))
        slab_1 = join(away[0], early[0])
        slab_0 = join(mine[0], jnp.where(cross, early[2], late[0]))
        first = join(jnp.where(cross, teacher, away[1]), early[1])
        other = join(away[2], early[2])
        fourth = join(mine[3], early[3])
        turn = lambda value, k: move(
            value, lambda z, c, x, y: (z, c, x, y - k) if c == 0 else None
        )
        around = [turn(first, k) for k in (1, 2, 3)]
        block_4 = move(
            jnp.where(cross, first, slab_1),
            lambda z, c, x, y: (z, c, x ^ 1, y) if c == 0 else (z, c, far(x), y),
        )
        block_5 = move(
            jnp.where(cross, block_4, first),
            lambda z, c, x, y: (z, c, x, y - 1) if c == 0 else (z, c, far(x), y),
        )
        block_7 = move(
            jnp.where(cross, block_4, fourth),
            lambda z, c, x, y: (z, c, x, y + 1) if c == 0 else (z, c, x ^ 1, y),
        )
        block_6 = move(
            jnp.where(cross, around[1], other),
            lambda z, c, x, y: (z, c, x ^ 1, y) if c == 0 else (z, c, far(x), y),
        )
        blocks = [
            jnp.where(cross, first, slab_0),
            jnp.where(cross, around[0], join(mine[1], late[1])),
            jnp.where(cross, around[1], join(mine[2], late[2])),
            jnp.where(cross, around[2], fourth),
            block_4,
            block_5,
            block_6,
            block_7,
        ]

    with jax.named_scope("normalize"):
        tile = 256
        height = 2 * BLK + PAD
        operand, rows = call(
            functools.partial(normalize_kernel, clip_total),
            "normalize",
            place,
            [*blocks, slab_0, slab_1, totals, partner, *turned],
            [pl.BlockSpec((tile, BLK), lambda i, p: (i, 0))] * 10 + [None] * 5,
            [((8, 2 * clips, BLK), BF), ((height, 2 * clips), BF)],
            [
                pl.BlockSpec((8, tile, BLK), lambda i, p: (0, i, 0)),
                pl.BlockSpec((height, tile), lambda i, p: (0, i)),
            ],
            grid=(2 * clips // tile,),
        )

    with jax.named_scope("reduce"):
        top, bottom = reduce_rows(place, rows, operand, clip_total)

    with jax.named_scope("spread"):
        tops, bottoms = {0: top}, {0: bottom}
        for k in range(1, 5):
            tops[-k] = z_shift(tops[1 - k], 1)
            bottoms[k] = z_shift(bottoms[k - 1], -1)
            if k < 4:
                bottoms[-k] = z_shift(bottoms[1 - k], 1)
                tops[k] = z_shift(tops[k - 1], -1)
        tops[4] = tops[-4]

    with jax.named_scope("direct"):
        (acc,) = direct_part(place, operand, (0, -1, 1), tops, bottoms, None, False)
        (acc,) = direct_part(place, operand, (-2, 2, -3, 3), tops, bottoms, acc, False)
        own_0, away_0, own_1, away_1 = direct_part(
            place, operand, (4,), tops, bottoms, acc, True
        )
        sent = own_1 + core_swap(away_1)
        wide = own_0 + core_swap(away_0)
        high = sent.astype(BF)
        low = (sent[clips:] - high[clips:].astype(F32)).astype(BF)
        arrived = move(join(high, low), lambda z, c, x, y: (z, c, (x + 2) % NX, y)).astype(F32)
        direct = wide[:clips] + arrived[:clips]
        sums = wide[clips:] + arrived[clips : clips + PAD] + arrived[clips + PAD :]

    with jax.named_scope("student_grad"):
        column = (x_hi * NY + y) * BLK
        center, scale = figures_of(
            lax.dynamic_slice_in_dim(totals, column, BLK, 1), clip_total
        )
        scaled = (mine[0].astype(F32) - center) * scale
        return scale * (direct - sums[0] - scaled * sums[1])


def solution(mesh):
    placed = (P("batch", "fi"), P("batch", ("fi", "fj")))
    return jax.shard_map(
        body, mesh=mesh, in_specs=placed, out_specs=P("batch", ("fi", "fj")), check_vma=False
    )
```

```python
import functools

import jax
import jax.numpy as jnp
from jax import lax
from jax.experimental import pallas as pl
from jax.experimental.pallas import tpu as pltpu
from jax.sharding import PartitionSpec as P

EPSILON = 1e-05
BF = jnp.bfloat16
F32 = jnp.float32
NZ, NC, NX, NY = 8, 2, 4, 4
BLK = 256
HALF = 128
PAD = 16
PARAMS = pltpu.CompilerParams(vmem_limit_bytes=28 * 1024 * 1024)


def move(value, target):
    flat = lambda z, c, x, y: (z % NZ * NC + c) * 16 + x % 2 * 8 + x // 2 * NY + y % NY
    pairs = []
    for z in range(NZ):
        for c in range(NC):
            for x in range(NX):
                for y in range(NY):
                    to = target(z, c, x, y)
                    if to is not None:
                        pairs.append((flat(z, c, x, y), flat(*to)))
    return lax.ppermute(value, ("batch", "fi", "fj"), pairs)


def z_shift(value, step):
    return move(value, lambda z, c, x, y: (z + step, c, x, y))


def z_swap(value, bit):
    return move(value, lambda z, c, x, y: (z ^ bit, c, x, y))


def core_swap(value):
    return move(value, lambda z, c, x, y: (z, 1 - c, x, y))


def far(x):
    return (x + 3) % NX if x % 2 == 0 else (x + 1) % NX


def dot(a, b, dims):
    return lax.dot_general(a, b, (dims, ((), ())), preferred_element_type=F32)


def whole(a):
    return pl.BlockSpec(a.shape, lambda i, *p, n=a.ndim: (0,) * n)


def call(kernel, name, scalars, operands, in_specs, shapes, out_specs=None, grid=(1,), flops=0):
    outs = [jax.ShapeDtypeStruct(s, d) for s, d in shapes]
    return pl.pallas_call(
        kernel,
        grid_spec=pltpu.PrefetchScalarGridSpec(
            num_scalar_prefetch=1,
            grid=grid,
            in_specs=[whole(a) if s is None else s for a, s in zip(operands, in_specs)],
            out_specs=out_specs or [whole(o) for o in outs],
        ),
        out_shape=outs,
        compiler_params=PARAMS,
        cost_estimate=pl.CostEstimate(flops=flops, bytes_accessed=1 << 20, transcendentals=0),
        name=name,
    )(scalars, *operands)


HIGHEST = lax.Precision.HIGHEST


def early_kernel(place, block, teacher, out):
    from_teacher = jnp.where(pl.program_id(0) == 1, place[1], 0) == 1
    out[0] = jnp.where(from_teacher, teacher[...], block[...])


def early_column(i, p):
    core, x_hi, y = p[1], p[2], p[3]
    other = (1 - x_hi) * NY
    mine = x_hi * NY
    third = jnp.where(core == 0, other + lax.rem(y + 2, NY), mine + y)
    last = mine + lax.rem(y + 3, NY)
    return jnp.where(i < 2, other + lax.rem(y + i, NY), jnp.where(i == 2, third, last))


def early_message(place, student, teacher):
    clips = student.shape[0]
    (out,) = call(
        early_kernel,
        "early_message",
        place,
        [student, teacher],
        [pl.BlockSpec((clips, BLK), lambda i, p: (0, early_column(i, p))), None],
        [((4, clips, BLK), BF)],
        [pl.BlockSpec((1, clips, BLK), lambda i, p: (i, 0, 0))],
        grid=(4,),
    )
    return out


def rows_kernel(place, slab_0, slab_1, rows, means):
    clips = slab_0.shape[0]
    for k, slab in enumerate((slab_0, slab_1)):
        wide = slab[...].astype(F32).T
        lanes = slice(k * BLK, k * BLK + BLK)
        rows[lanes] = wide.astype(BF)
        mean = jnp.sum(wide, 1, keepdims=True) * (1.0 / clips)
        means[lanes] = jnp.broadcast_to(mean, (BLK, HALF))
    line = lax.broadcasted_iota(jnp.int32, (PAD, clips), 0)
    rows[2 * BLK :] = jnp.where(line == 0, 1.0, 0.0).astype(BF)


def sums_kernel(place, early, late, slab_0, slab_1, out):
    def add(start, values):
        values = values.astype(F32)
        part = jnp.concatenate(
            [jnp.sum(values, 0, keepdims=True), jnp.sum(values * values, 0, keepdims=True)], 0
        )
        lanes = slice(start, start + BLK)
        first = pl.program_id(0) == 0
        out[:, lanes] = jnp.where(first, part, out[:, lanes] + part)

    for k in range(4):
        add(k * BLK, early[k])
        add((4 + k) * BLK, late[k])
    add(8 * BLK, slab_0[...])
    add(9 * BLK, slab_1[...])


def figures_of(sums, squares, clip_total):
    center = jnp.sum(sums, 0, keepdims=True) / clip_total
    scale = lax.rsqrt(squares / clip_total - center * center + EPSILON)
    return center, scale


def normalize_kernel(clip_total, place, early, late, sums, squares, operand, column, total):
    for half, blocks in enumerate((early, late)):
        for piece in range(NZ):
            start = half * 4 * BLK + piece * HALF
            lanes = slice(start, start + HALF)
            center, scale = figures_of(sums[:, lanes], squares[:, lanes], clip_total)
            inner = piece % 2 * HALF
            values = blocks[piece // 2, :, inner : inner + HALF].astype(F32)
            values = ((values - center) * scale).astype(BF)
            place_lanes = slice(half * HALF, half * HALF + HALF)
            operand[piece, :, place_lanes] = values
            part = jnp.sum(values.astype(F32), 0, keepdims=True)
            first = pl.program_id(0) == 0
            old = total[piece : piece + 1, place_lanes]
            total[piece : piece + 1, place_lanes] = jnp.where(first, part, old + part)
    column[...] = total[...]


def centered(rows, means, piece):
    part = dot(rows[...], piece[0], ((1,), (0,)))
    return part[: 2 * BLK] - means[...] * part[2 * BLK : 2 * BLK + 1]


def step_kernel(count, has_received, place, rows, means, *refs):
    pieces, refs = refs[:count], refs[count:]
    received, outs = (refs[:count], refs[count:]) if has_received else (None, refs)
    for k in range(count):
        value = centered(rows, means, pieces[k])
        if has_received:
            value = value + received[k][...].astype(F32)
        outs[k][...] = value.astype(BF)


def gradient_kernel(
    clip_total, place, rows, means, early, late, sums, squares, *refs
):
    received, (top, bottom) = refs[:4], refs[4:]
    z, core = place[0], place[1]
    clips = rows.shape[1]
    row_lanes = slice(8 * BLK, 10 * BLK)
    line = lax.broadcasted_iota(jnp.int32, (NZ, 1), 0)

    def figures(lanes):
        center, scale = figures_of(sums[:, lanes], squares[:, lanes], clip_total)
        away = sums[:, lanes] * (1.0 / clips) - center
        return away, jnp.where(line == 0, scale, 0.0)

    def outer(a, b):
        return lax.dot_general(
            a, b, (((0,), (0,)), ((), ())), precision=HIGHEST, preferred_element_type=F32
        )

    row_away, row_scale = figures(row_lanes)
    for half, piece in enumerate((early, late)):
        start = pl.multiple_of(z * HALF + half * 4 * BLK, HALF)
        away, scale = figures(pl.ds(start, HALF))
        value = centered(rows, means, piece)
        value = value + received[2 * half][...].astype(F32)
        value = value + received[2 * half + 1][...].astype(F32)
        value = value + outer(row_away, away) * float(clips)
        value = value * outer(row_scale, scale) * (1.0 / clip_total)
        lanes = slice(half * HALF, half * HALF + HALF)
        upper = value[:BLK]
        if half == 0:
            row = lax.broadcasted_iota(jnp.int32, (BLK, HALF), 0)
            col = lax.broadcasted_iota(jnp.int32, (BLK, HALF), 1)
            diagonal = row == col + z * HALF
            on = jnp.where(core == 0, 2.0 * (upper - 1.0), 0.0)
            upper = jnp.where(diagonal, on, upper)
        top[:, lanes] = upper.astype(BF)
        bottom[:, lanes] = value[BLK:].astype(BF)


def piece_spec(blocks, offset):
    def index(i, p):
        piece = lax.rem(p[0] + (offset + NZ), NZ)
        return piece // 2, 0, lax.rem(piece, 2)

    return pl.BlockSpec((1, blocks.shape[1], HALF), index)


def reduce_rows(place, rows, means, early, late):
    height = 2 * BLK
    flops = 2 * rows.shape[0] * rows.shape[1] * HALF

    def step(blocks, offsets, received):
        count = len(offsets)
        operands = [rows, means, *[blocks] * count, *(received or [])]
        specs = [None] * 2 + [piece_spec(blocks, k) for k in offsets]
        specs += [None] * len(received or [])
        return call(
            functools.partial(step_kernel, count, received is not None),
            "ring_step",
            place,
            operands,
            specs,
            [((height, HALF), BF)] * count,
            flops=count * flops,
        )

    right, left = step(early, (4, -3), None)
    a = [z_shift(right, 1), z_shift(left, -1)]
    left, right = step(late, (-4, 3), None)
    b = [z_shift(left, -1), z_shift(right, 1)]
    for hop in (1, 2):
        right, left = step(early, (4 - hop, hop - 3), a)
        a = [z_shift(right, 1), z_shift(left, -1)]
        left, right = step(late, (hop - 4, 3 - hop), b)
        b = [z_shift(left, -1), z_shift(right, 1)]
    (right,) = step(early, (1,), a[:1])
    a = [z_shift(right, 1), a[1]]
    (left,) = step(late, (-1,), b[:1])
    b = [z_shift(left, -1), b[1]]
    return a + b


def gradient(place, rows, means, early, late, sums, squares, received, clip_total):
    operands = [rows, means, early, late, sums, squares, *received]
    specs = [None, None, piece_spec(early, 0), piece_spec(late, 0)] + [None] * 6
    return call(
        functools.partial(gradient_kernel, clip_total),
        "gradient",
        place,
        operands,
        specs,
        [((BLK, BLK), BF)] * 2,
    )


def direct_kernel(offsets, has_acc, last, clip_total, place, *refs):
    count = len(offsets)
    pieces, tops, bottoms = refs[:count], refs[count : 2 * count], refs[2 * count : 3 * count]
    column = refs[3 * count]
    acc = refs[3 * count + 1] if has_acc else None
    outs = refs[3 * count + (2 if has_acc else 1) :]
    clips = pieces[0].shape[1]
    ones = jnp.ones((PAD, BLK), BF)
    z, core = place[0], place[1]
    row = lax.broadcasted_iota(jnp.int32, (BLK, BLK), 0)
    col = lax.broadcasted_iota(jnp.int32, (BLK, BLK), 1)
    line = lax.broadcasted_iota(jnp.int32, (PAD, BLK), 0)
    for half in (1, 0):
        lanes = slice(half * BLK, half * BLK + BLK)
        total = acc[:clips, lanes] if has_acc else None
        sums = acc[clips:, lanes] if has_acc else None
        for k in range(count):
            index = lax.rem(z + (offsets[k] + NZ), NZ)
            grad = tops[k][...] if half == 0 else bottoms[k][...]
            product = dot(pieces[k][0], grad, ((1,), (1,)))
            total = product if total is None else total + product
            wide = grad.astype(F32)
            square = wide * wide
            if half == 0:
                limit = jnp.where(core == 0, HALF, 0)
                diagonal = jnp.where(col < limit, col + index * HALF, -1) == row
                square = jnp.where(diagonal, wide * (wide * 0.5 + 1.0), square)
            high = square.astype(BF)
            low = (square - high.astype(F32)).astype(BF)
            product = dot(ones, high, ((1,), (1,))) + dot(ones, low, ((1,), (1,)))
            mean = column[pl.ds(index, 1), :] * (1.0 / clip_total)
            mean_high = mean.astype(BF)
            mean_low = (mean - mean_high.astype(F32)).astype(BF)
            means = jnp.where(
                line == 0,
                mean_high.astype(F32),
                jnp.where(line == 1, mean_low.astype(F32), 0.0),
            ).astype(BF)
            both = dot(means, grad, ((1,), (1,))) + jnp.where(line == 2, product, 0.0)
            sums = both if sums is None else sums + both
        if last:
            middle = clips // 2
            for part in range(2):
                out = outs[2 * half + part]
                out[:middle] = total[part * middle : part * middle + middle]
                out[middle:] = sums
        else:
            outs[0][:clips, lanes] = total
            outs[0][clips:, lanes] = sums


def direct_part(place, operand, column, offsets, tops, bottoms, acc, last, clip_total):
    clips = operand.shape[1]
    operands = [operand] * len(offsets)
    specs = [
        pl.BlockSpec(
            (1, *operand.shape[1:]), lambda i, p, k=k: (lax.rem(p[0] + (k + NZ), NZ), 0, 0)
        )
        for k in offsets
    ]
    more = [tops[k] for k in offsets] + [bottoms[k] for k in offsets] + [column]
    more += [] if acc is None else [acc]
    if last:
        shapes = [((clips // 2 + PAD, BLK), F32)] * 4
    else:
        shapes = [((clips + PAD, 2 * BLK), F32)]
    return call(
        functools.partial(direct_kernel, offsets, acc is not None, last, clip_total),
        "direct_part",
        place,
        operands + more,
        specs + [None] * len(more),
        shapes,
        flops=len(offsets) * 4 * clips * BLK * BLK,
    )


def body(student, teacher):
    clips = student.shape[0]
    clip_total = clips * NZ * NC
    batch = lax.axis_index("batch")
    z, core = batch // NC, batch % NC
    fj = lax.axis_index("fj")
    x_hi, y = fj // NY, fj % NY
    place = jnp.stack([z, core, x_hi, y]).astype(jnp.int32)
    cross = core == 0

    def cut(hi, step):
        column = (hi * NY + (y + step) % NY) * BLK
        return lax.dynamic_slice_in_dim(student, column, BLK, 1)

    def join(mine, others):
        return jnp.concatenate([mine, others], 0)

    with jax.named_scope("operand_blocks"):
        early = core_swap(early_message(place, student, teacher))
        mine = [cut(x_hi, k) for k in range(4)]
        away = [cut(1 - x_hi, k) for k in range(3)]
        late = core_swap(jnp.stack(mine[:3]))
        slab_1 = join(away[0], early[0])
        slab_0 = join(mine[0], jnp.where(cross, early[2], late[0]))
        first = join(jnp.where(cross, teacher, away[1]), early[1])
        other = join(away[2], early[2])
        fourth = join(mine[3], early[3])
        turn = lambda value, k: move(
            value, lambda z, c, x, y: (z, c, x, y - k) if c == 0 else None
        )
        around = [turn(first, k) for k in (1, 2, 3)]
        block_4 = move(
            jnp.where(cross, first, slab_1),
            lambda z, c, x, y: (z, c, x ^ 1, y) if c == 0 else (z, c, far(x), y),
        )
        block_5 = move(
            jnp.where(cross, block_4, first),
            lambda z, c, x, y: (z, c, x, y - 1) if c == 0 else (z, c, far(x), y),
        )
        block_7 = move(
            jnp.where(cross, block_4, fourth),
            lambda z, c, x, y: (z, c, x, y + 1) if c == 0 else (z, c, x ^ 1, y),
        )
        block_6 = move(
            jnp.where(cross, around[1], other),
            lambda z, c, x, y: (z, c, x ^ 1, y) if c == 0 else (z, c, far(x), y),
        )
        early_blocks = jnp.stack(
            [
                jnp.where(cross, first, slab_0),
                jnp.where(cross, around[0], join(mine[1], late[1])),
                jnp.where(cross, around[1], join(mine[2], late[2])),
                jnp.where(cross, around[2], fourth),
            ]
        )
        late_blocks = jnp.stack([block_4, block_5, block_6, block_7])

    with jax.named_scope("rows"):
        rows, means = call(
            rows_kernel,
            "rows",
            place,
            [slab_0, slab_1],
            [None] * 2,
            [((2 * BLK + PAD, 2 * clips), BF), ((2 * BLK, HALF), F32)],
        )

    with jax.named_scope("reduce"):
        received = reduce_rows(place, rows, means, early_blocks, late_blocks)

    tile = 256
    grid = (2 * clips // tile,)
    blocks_spec = pl.BlockSpec((4, tile, BLK), lambda i, p: (0, i, 0))
    with jax.named_scope("statistics"):
        (totals,) = call(
            sums_kernel,
            "column_sums",
            place,
            [early_blocks, late_blocks, slab_0, slab_1],
            [blocks_spec] * 2 + [pl.BlockSpec((tile, BLK), lambda i, p: (i, 0))] * 2,
            [((2, 10 * BLK), F32)],
            grid=grid,
        )
        sums, squares = totals[:1], totals[1:]
        for bit in (1, 2, 4):
            arrived = z_swap(join(sums, squares), bit)
            sums = join(sums, arrived[:bit])
            squares = squares + arrived[bit:]

    with jax.named_scope("normalize"):
        operand, column = normalize(place, early_blocks, late_blocks, sums, squares, clip_total)
        for bit in (1, 2, 4):
            column = column + z_swap(column, bit)

    with jax.named_scope("gradient"):
        top, bottom = gradient(
            place, rows, means, early_blocks, late_blocks, sums, squares, received, clip_total
        )

    with jax.named_scope("spread"):
        tops, bottoms = {0: top}, {0: bottom}
        for k in range(1, 5):
            tops[-k] = z_shift(tops[1 - k], 1)
            bottoms[k] = z_shift(bottoms[k - 1], -1)
            if k < 4:
                bottoms[-k] = z_shift(bottoms[1 - k], 1)
                tops[k] = z_shift(tops[k - 1], -1)
        tops[4] = tops[-4]

    with jax.named_scope("direct"):
        part = lambda offsets, acc, last: direct_part(
            place, operand, column, offsets, tops, bottoms, acc, last, clip_total
        )
        (acc,) = part((0, -1, 1), None, False)
        (acc,) = part((-2, 2, -3, 3), acc, False)
        own_0, away_0, own_1, away_1 = part((4,), acc, True)
        sent = own_1 + core_swap(away_1)
        wide = own_0 + core_swap(away_0)
        high = sent.astype(BF)
        low = (sent[clips:] - high[clips:].astype(F32)).astype(BF)
        arrived = move(join(high, low), lambda z, c, x, y: (z, c, (x + 2) % NX, y)).astype(F32)
        direct = wide[:clips] + arrived[:clips]
        ends = wide[clips:] + arrived[clips : clips + PAD] + arrived[clips + PAD :]

    with jax.named_scope("student_grad"):
        lanes = slice(8 * BLK, 9 * BLK)
        center, scale = figures_of(sums[:, lanes], squares[:, lanes], clip_total)
        scaled = (mine[0].astype(F32) - center) * scale
        return scale * (direct - (ends[0] + ends[1]) - scaled * ends[2])


def normalize(place, early, late, sums, squares, clip_total):
    clips = early.shape[1]
    tile = 256
    blocks_spec = pl.BlockSpec((4, tile, BLK), lambda i, p: (0, i, 0))
    outs = [
        jax.ShapeDtypeStruct((NZ, clips, BLK), BF),
        jax.ShapeDtypeStruct((NZ, BLK), F32),
    ]
    return pl.pallas_call(
        functools.partial(normalize_kernel, clip_total),
        grid_spec=pltpu.PrefetchScalarGridSpec(
            num_scalar_prefetch=1,
            grid=(clips // tile,),
            in_specs=[blocks_spec, blocks_spec, whole(sums), whole(squares)],
            out_specs=[pl.BlockSpec((NZ, tile, BLK), lambda i, p: (0, i, 0)), whole(outs[1])],
            scratch_shapes=[pltpu.VMEM((NZ, BLK), F32)],
        ),
        out_shape=outs,
        compiler_params=PARAMS,
        name="normalize",
    )(place, early, late, sums, squares)


def solution(mesh):
    placed = (P("batch", "fi"), P("batch", ("fi", "fj")))
    return jax.shard_map(
        body, mesh=mesh, in_specs=placed, out_specs=P("batch", ("fi", "fj")), check_vma=False
    )
```

```python
import functools

import jax
import jax.numpy as jnp
from jax import lax
from jax.experimental import pallas as pl
from jax.experimental.pallas import tpu as pltpu
from jax.sharding import PartitionSpec as P

EPSILON = 1e-05
BF = jnp.bfloat16
F32 = jnp.float32
NZ, NC, NX, NY = 8, 2, 4, 4
BLK = 256
HALF = 128
PACK = 64
PAD = 16
PARAMS = pltpu.CompilerParams(vmem_limit_bytes=28 * 1024 * 1024)


def move(value, target):
    flat = lambda z, c, x, y: (z % NZ * NC + c) * 16 + x % 2 * 8 + x // 2 * NY + y % NY
    pairs = []
    for z in range(NZ):
        for c in range(NC):
            for x in range(NX):
                for y in range(NY):
                    to = target(z, c, x, y)
                    if to is not None:
                        pairs.append((flat(z, c, x, y), flat(*to)))
    return lax.ppermute(value, ("batch", "fi", "fj"), pairs)


def z_shift(value, step):
    return move(value, lambda z, c, x, y: (z + step, c, x, y))


def z_swap(value, bit):
    return move(value, lambda z, c, x, y: (z ^ bit, c, x, y))


def core_swap(value):
    return move(value, lambda z, c, x, y: (z, 1 - c, x, y))


def far(x):
    return (x + 3) % NX if x % 2 == 0 else (x + 1) % NX


def dot(a, b, dims):
    return lax.dot_general(a, b, (dims, ((), ())), preferred_element_type=F32)


def whole(a):
    return pl.BlockSpec(a.shape, lambda i, *p, n=a.ndim: (0,) * n)


def call(
    kernel,
    name,
    scalars,
    operands,
    in_specs,
    shapes,
    out_specs=None,
    grid=(1,),
    flops=0,
    nbytes=1 << 20,
    after=(),
):
    outs = [jax.ShapeDtypeStruct(s, d) for s, d in shapes]
    first, count = 1 + len(operands), len(after)

    def body(*refs):
        kernel(*refs[:first], *refs[first + count :])

    resident = pl.BlockSpec(memory_space=pltpu.VMEM)
    place_whole = (lambda a: resident) if grid == (1,) else whole
    specs = [place_whole(a) if s is None else s for a, s in zip(operands, in_specs)]
    return pl.pallas_call(
        body,
        grid_spec=pltpu.PrefetchScalarGridSpec(
            num_scalar_prefetch=1,
            grid=grid,
            in_specs=specs + [pl.BlockSpec(memory_space=pl.ANY)] * count,
            out_specs=out_specs or [place_whole(o) for o in outs],
        ),
        out_shape=outs,
        compiler_params=PARAMS,
        cost_estimate=pl.CostEstimate(flops=flops, bytes_accessed=nbytes, transcendentals=0),
        name=name,
    )(scalars, *operands, *after)


HIGHEST = lax.Precision.HIGHEST


def stage_kernel(place, student, distant, *refs):
    teacher, (keep, send) = refs[:NZ], refs[NZ:]
    cross = place[1] == 0
    for k in range(NZ):
        turned = lax.rem(place[3] + k, NY)
        source, column = (student, place[2] * NY + turned) if k < NY else (distant, turned)
        a = source[:, pl.ds(pl.multiple_of(column * BLK, BLK), BLK)]
        b = teacher[k][...]
        keep[k] = jnp.where(cross, b, a)
        send[k] = jnp.where(cross, a, b)


def stage(place, student, distant, teacher, after):
    operands = [student, distant, *teacher]
    return call(
        stage_kernel,
        "stage",
        place,
        operands,
        [None] * len(operands),
        [((NZ, student.shape[0], BLK), BF)] * 2,
        nbytes=8 << 20,
        after=after,
    )


def prepare_kernel(place, half, slab_0, slab_1, far_half, slabs):
    far_half[...] = half[...]
    slabs[0] = slab_0[...]
    slabs[1] = slab_1[...]


def prepare(place, student):
    clips = student.shape[0]
    tile = 128
    width = NY * BLK
    return call(
        prepare_kernel,
        "prepare",
        place,
        [student] * 3,
        [
            pl.BlockSpec((tile, width), lambda i, p: (i, 1 - p[2])),
            pl.BlockSpec((tile, BLK), lambda i, p: (i, p[2] * NY + p[3])),
            pl.BlockSpec((tile, BLK), lambda i, p: (i, (1 - p[2]) * NY + p[3])),
        ],
        [((clips, width), BF), ((2, clips, BLK), BF)],
        [
            pl.BlockSpec((tile, width), lambda i, p: (i, 0)),
            pl.BlockSpec((2, tile, BLK), lambda i, p: (0, i, 0)),
        ],
        grid=(clips // tile,),
    )


def rows_kernel(place, slabs, other_slabs, rows, means):
    clips = slabs.shape[1]
    for k in range(2):
        lines = slice(k * BLK, k * BLK + BLK)
        total = 0.0
        for part, source in enumerate((slabs, other_slabs)):
            wide = source[k].astype(F32).T
            rows[lines, part * clips : part * clips + clips] = wide.astype(BF)
            total = total + jnp.sum(wide, 1, keepdims=True)
        means[lines] = jnp.broadcast_to(total * (0.5 / clips), (BLK, BLK))
    line = lax.broadcasted_iota(jnp.int32, (PAD, 2 * clips), 0)
    rows[2 * BLK :] = jnp.where(line == 0, 1.0, 0.0).astype(BF)


def sums_kernel(place, keep, send, slabs, keep_total, send_total):
    for target, blocks in ((keep_total, keep), (send_total, send)):
        for k in range(10):
            lanes = slice(k * BLK, k * BLK + BLK)
            if k >= NZ and target is send_total:
                target[:, lanes] = keep_total[:, lanes]
                continue
            values = (blocks[k] if k < NZ else slabs[k - NZ]).astype(F32)
            target[0:1, lanes] = jnp.sum(values, 0, keepdims=True)
            target[1:2, lanes] = jnp.sum(values * values, 0, keepdims=True)


def column_sums(place, keep, send, slabs):
    operands = [keep, send, slabs]
    return call(
        sums_kernel,
        "column_sums",
        place,
        operands,
        [None] * 3,
        [((2, 10 * BLK), F32)] * 2,
        nbytes=6 << 20,
    )


def pack_kernel(place, own, other, out):
    total = own[...] + other[...]
    lines = [
        total[kind : kind + 1, n * HALF : n * HALF + HALF] for kind in range(2) for n in range(20)
    ]
    rest = jnp.concatenate(lines, 0)
    terms = []
    for _ in range(3):
        term = rest.astype(BF).astype(F32)
        terms.append(term)
        rest = rest - term
    terms.append(jnp.zeros((8, HALF), F32))
    lines = jnp.concatenate(terms, 0).astype(BF)
    out[...] = jnp.concatenate([lines[:PACK], lines[PACK:]], 1)


def unpack_kernel(place, *refs):
    packed, (sums, squares) = refs[:NZ], refs[NZ:]
    square_lines = 0.0
    for k in range(NZ):
        wide = packed[k][packed[k].shape[0] - PACK :].astype(F32)
        wide = jnp.concatenate([wide[:, :HALF], wide[:, HALF:]], 0)
        lines = wide[:40] + wide[40:80] + wide[80:120]
        for n in range(20):
            sums[k : k + 1, n * HALF : n * HALF + HALF] = lines[n : n + 1]
        square_lines = square_lines + lines[20:]
    for n in range(20):
        squares[:, n * HALF : n * HALF + HALF] = square_lines[n : n + 1]


def figures_of(sums, squares, clip_total):
    center = jnp.sum(sums, 0, keepdims=True) / clip_total
    scale = lax.rsqrt(squares / clip_total - center * center + EPSILON)
    return center, scale


def centered(rows, means, blocks, index):
    clips = blocks[0].shape[1]
    part = dot(rows[:, :clips], blocks[0][index], ((1,), (0,)))
    part = part + dot(rows[:, clips:], blocks[1][index], ((1,), (0,)))
    return part[: 2 * BLK] - means[...] * part[2 * BLK : 2 * BLK + 1]


def far_kernel(place, rows, means, own, other, packed, top, bottom):
    index = lax.rem(place[0] + 4, NZ)
    value = centered(rows, means, (own, other), index).astype(BF)
    top[:BLK] = value[:BLK]
    bottom[:BLK] = value[BLK:]
    top[BLK:] = packed[...]
    bottom[BLK:] = packed[...]


def product_kernel(offsets, place, rows, means, own, other, *outs):
    for k, out in zip(offsets, outs):
        index = lax.rem(place[0] + (k + NZ), NZ)
        out[...] = centered(rows, means, (own, other), index)


def gradient_kernel(
    clip_total, place, own, sums, squares, from_left, from_right, top, bottom
):
    z, core = place[0], place[1]
    clips = clip_total // NZ
    line = lax.broadcasted_iota(jnp.int32, (NZ, 1), 0)

    def figures(lanes):
        center, scale = figures_of(sums[:, lanes], squares[:, lanes], clip_total)
        away = sums[:, lanes] * (1.0 / clips) - center
        return away, jnp.where(line == 0, scale, 0.0), scale

    def outer(a, b):
        return lax.dot_general(
            a, b, (((0,), (0,)), ((), ())), precision=HIGHEST, preferred_element_type=F32
        )

    row_away, row_scale, _ = figures(slice(8 * BLK, 10 * BLK))
    away, scale, column_scale = figures(pl.ds(pl.multiple_of(z * BLK, BLK), BLK))
    height = 2 * BLK
    value = own[...] + from_left[:height].astype(F32) + from_right[:height].astype(F32)
    value = value + outer(row_away, away) * float(clips)
    value = value * outer(row_scale, scale) * (1.0 / clip_total)
    upper = value[:BLK]
    row = lax.broadcasted_iota(jnp.int32, (BLK, BLK), 0)
    col = lax.broadcasted_iota(jnp.int32, (BLK, BLK), 1)
    diagonal = row == col + z * BLK
    on = jnp.where(core == 0, 2.0 * (upper - 1.0), 0.0)
    upper = jnp.where(diagonal, on, upper)
    top[...] = (upper * column_scale).astype(BF)
    bottom[...] = (value[BLK:] * column_scale).astype(BF)


def reduce_rows(place, rows, means, blocks, packed):
    height = 2 * BLK
    flops = 2 * rows.shape[0] * rows.shape[1] * BLK

    def products(kernel, extra, count, shapes):
        operands = [rows, means, *blocks, *extra]
        return call(
            kernel,
            "products",
            place,
            operands,
            [None] * len(operands),
            shapes,
            flops=count * flops,
            nbytes=(2 + count) << 20,
        )

    def wide(*offsets):
        kernel = functools.partial(product_kernel, offsets)
        return products(kernel, (), len(offsets), [((height, BLK), F32)] * len(offsets))

    top, bottom = products(far_kernel, [packed], 1, [((BLK + PACK, BLK), BF)] * 2)
    from_left, from_right = z_shift(top, 1), z_shift(bottom, -1)
    gathered = [from_left, from_right]
    ahead, behind = wide(3, -3)
    own, *ready = wide(0, 2, -2, 1, -1)

    def add(part, arrived):
        return (part + arrived.astype(F32)).astype(BF)

    right = [add(ahead[:BLK], from_left[:BLK]), ahead[BLK:].astype(BF), from_left[BLK:]]
    left = [behind[:BLK].astype(BF), add(behind[BLK:], from_right[:BLK]), from_right[BLK:]]
    for hop in range(3):
        from_left = z_shift(jnp.concatenate(right, 0), 1)
        from_right = z_shift(jnp.concatenate(left, 0), -1)
        gathered += [from_left, from_right]
        if hop < 2:
            ahead, behind = ready[2 * hop : 2 * hop + 2]
            right = [add(ahead, from_left[:height]), from_left[height:]]
            left = [add(behind, from_right[:height]), from_right[height:]]
    return own, from_left, from_right, gathered[:-1]


def gradient(place, own, sums, squares, from_left, from_right, clip_total):
    operands = [own, sums, squares, from_left, from_right]
    return call(
        functools.partial(gradient_kernel, clip_total),
        "gradient",
        place,
        operands,
        [None] * 5,
        [((BLK, BLK), BF)] * 2,
    )


def direct_kernel(offsets, has_acc, last, clip_total, place, *refs):
    count = len(offsets)
    blocks, tops, bottoms = refs[:2], refs[2 : 2 + count], refs[2 + count : 2 + 2 * count]
    refs = refs[2 + 2 * count :]
    all_sums, all_squares = refs[:2]
    acc = refs[2] if has_acc else None
    outs = refs[3 if has_acc else 2 :]
    middle = blocks[0].shape[1]
    clips = 2 * middle
    ones = jnp.ones((PAD, BLK), BF)
    z, core = place[0], place[1]
    row = lax.broadcasted_iota(jnp.int32, (BLK, BLK), 0)
    col = lax.broadcasted_iota(jnp.int32, (BLK, BLK), 1)
    line = lax.broadcasted_iota(jnp.int32, (PAD, BLK), 0)
    total = [acc[:clips, h * BLK : h * BLK + BLK] if has_acc else None for h in range(2)]
    ends = [acc[clips:, h * BLK : h * BLK + BLK] if has_acc else None for h in range(2)]
    for k in range(count):
        index = lax.rem(z + (offsets[k] + NZ), NZ)
        lanes = pl.ds(pl.multiple_of(index * BLK, BLK), BLK)
        center, scale = figures_of(all_sums[:, lanes], all_squares[:, lanes], clip_total)
        unscale = 1.0 / scale
        means = jnp.zeros((PAD, BLK), F32)
        for n in range(3):
            high = center.astype(BF).astype(F32)
            means = jnp.where(line == n, high, means)
            center = center - high
        means = means.astype(BF)
        block = jnp.concatenate([blocks[0][index], blocks[1][index]], 0)
        for half in (1, 0):
            grad = tops[k][...] if half == 0 else bottoms[k][...]
            product = dot(block, grad, ((1,), (1,)))
            total[half] = product if total[half] is None else total[half] + product
            wide = grad.astype(F32) * unscale
            square = wide * wide
            if half == 0:
                diagonal = row == col + (index + core) * BLK
                square = jnp.where(diagonal, wide * (wide * 0.5 + 1.0), square)
            high = square.astype(BF)
            low = (square - high.astype(F32)).astype(BF)
            product = dot(ones, high, ((1,), (1,))) + dot(ones, low, ((1,), (1,)))
            both = jnp.where(line < 3, dot(means, grad, ((1,), (1,))), product)
            ends[half] = both if ends[half] is None else ends[half] + both
    for half in range(2):
        if last:
            mean = jnp.sum(ends[half][:3], 0, keepdims=True)
            for part in range(2):
                out = outs[2 * half + part]
                out[:middle] = total[half][part * middle : part * middle + middle] - mean
                out[middle:] = ends[half]
        else:
            outs[0][:clips, half * BLK : half * BLK + BLK] = total[half]
            outs[0][clips:, half * BLK : half * BLK + BLK] = ends[half]


def direct_part(place, blocks, sums, squares, offsets, tops, bottoms, acc, last, clip_total):
    clips = 2 * blocks[0].shape[1]
    more = [tops[k] for k in offsets] + [bottoms[k] for k in offsets] + [sums, squares]
    more += [] if acc is None else [acc]
    if last:
        shapes = [((clips // 2 + PAD, BLK), F32)] * 4
    else:
        shapes = [((clips + PAD, 2 * BLK), F32)]
    return call(
        functools.partial(direct_kernel, offsets, acc is not None, last, clip_total),
        "direct_part",
        place,
        [*blocks, *more],
        [None] * (2 + len(more)),
        shapes,
        flops=len(offsets) * 4 * clips * BLK * BLK,
        nbytes=8 << 20,
    )


def body(student, teacher):
    clips = student.shape[0]
    clip_total = clips * NZ * NC
    batch = lax.axis_index("batch")
    z, core = batch // NC, batch % NC
    fj = lax.axis_index("fj")
    x_hi, y = fj // NY, fj % NY
    place = jnp.stack([z, core, x_hi, y]).astype(jnp.int32)

    def join(mine, others):
        return jnp.concatenate([mine, others], 0)

    with jax.named_scope("operand_blocks"):

        def turn(value, k):
            return move(value, lambda z, c, x, y: (z, c, x, y - k))

        def partner(value):
            return move(value, lambda z, c, x, y: (z, c, x ^ 1, y))

        around = [teacher] + [turn(teacher, k) for k in (1, 2, 3)]
        across = partner(teacher)
        far_half, slabs = prepare(place, student)
        distant = move(far_half, lambda z, c, x, y: (z, c, far(x), y))
        other_slabs = core_swap(slabs)
        across = [across, turn(across, 1), partner(around[2]), turn(across, 3)]
        teacher_blocks = around + across

    with jax.named_scope("rows"):
        rows, means = call(
            rows_kernel,
            "rows",
            place,
            [slabs, other_slabs],
            [None] * 2,
            [((2 * BLK + PAD, 2 * clips), BF), ((2 * BLK, BLK), F32)],
        )

    with jax.named_scope("stage"):
        keep, send = stage(place, student, distant, teacher_blocks, [rows])
        blocks = keep, core_swap(send)

    with jax.named_scope("statistics"):
        own_sums, other_sums = column_sums(place, keep, send, slabs)
        (packed,) = call(
            pack_kernel,
            "pack",
            place,
            [own_sums, core_swap(other_sums)],
            [None] * 2,
            [((PACK, BLK), BF)],
        )

    with jax.named_scope("reduce"):
        own, right, left, gathered = reduce_rows(place, rows, means, blocks, packed)

    with jax.named_scope("statistics"):
        sums, squares = call(
            unpack_kernel,
            "unpack",
            place,
            [packed, *gathered],
            [None] * NZ,
            [((NZ, 10 * BLK), F32), ((1, 10 * BLK), F32)],
        )

    with jax.named_scope("gradient"):
        top, bottom = gradient(place, own, sums, squares, right, left, clip_total)

    with jax.named_scope("spread"):
        tops, bottoms = {0: top}, {0: bottom}
        for k in range(1, 5):
            tops[-k] = z_shift(tops[1 - k], 1)
            bottoms[k] = z_shift(bottoms[k - 1], -1)
            if k < 4:
                bottoms[-k] = z_shift(bottoms[1 - k], 1)
                tops[k] = z_shift(tops[k - 1], -1)
        tops[4] = tops[-4]

    with jax.named_scope("direct"):
        part = lambda offsets, acc, last: direct_part(
            place,
            blocks,
            sums,
            squares,
            offsets,
            tops,
            bottoms,
            acc,
            last,
            clip_total,
        )
        (acc,) = part((0, -1, 1), None, False)
        (acc,) = part((-2, 2, -3, 3), acc, False)
        own_0, away_0, own_1, away_1 = part((4,), acc, True)
        sent = own_1 + core_swap(away_1)
        wide = own_0 + core_swap(away_0)
        high = sent.astype(BF)
        low = (sent[clips:] - high[clips:].astype(F32)).astype(BF)
        arrived = move(join(high, low), lambda z, c, x, y: (z, c, (x + 2) % NX, y)).astype(F32)
        direct = wide[:clips] + arrived[:clips]
        product = wide[clips + 3] + arrived[clips + 3] + arrived[clips + PAD + 3]

    with jax.named_scope("student_grad"):
        lanes = slice(8 * BLK, 9 * BLK)
        center, scale = figures_of(sums[:, lanes], squares[:, lanes], clip_total)
        scaled = (slabs[0].astype(F32) - center) * scale
        return scale * (direct - scaled * product)


def solution(mesh):
    placed = (P("batch", "fi"), P("batch", ("fi", "fj")))
    return jax.shard_map(
        body, mesh=mesh, in_specs=placed, out_specs=P("batch", ("fi", "fj")), check_vma=False
    )
```

```python
import functools

import jax
import jax.numpy as jnp
from jax import lax
from jax.experimental import pallas as pl
from jax.experimental.pallas import tpu as pltpu
from jax.sharding import PartitionSpec as P

EPSILON = 1e-05
BF = jnp.bfloat16
F32 = jnp.float32
NZ, NC, NX, NY = 8, 2, 4, 4
BLK = 256
HALF = 128
PACK = 64
PAD = 16
PARAMS = pltpu.CompilerParams(vmem_limit_bytes=28 * 1024 * 1024)


def move(value, target):
    flat = lambda z, c, x, y: (z % NZ * NC + c) * 16 + x % 2 * 8 + x // 2 * NY + y % NY
    pairs = []
    for z in range(NZ):
        for c in range(NC):
            for x in range(NX):
                for y in range(NY):
                    to = target(z, c, x, y)
                    if to is not None:
                        pairs.append((flat(z, c, x, y), flat(*to)))
    return lax.ppermute(value, ("batch", "fi", "fj"), pairs)


def z_shift(value, step):
    return move(value, lambda z, c, x, y: (z + step, c, x, y))


def z_swap(value, bit):
    return move(value, lambda z, c, x, y: (z ^ bit, c, x, y))


def core_swap(value):
    return move(value, lambda z, c, x, y: (z, 1 - c, x, y))


def far(x):
    return (x + 3) % NX if x % 2 == 0 else (x + 1) % NX


def dot(a, b, dims):
    return lax.dot_general(a, b, (dims, ((), ())), preferred_element_type=F32)


def whole(a):
    return pl.BlockSpec(a.shape, lambda i, *p, n=a.ndim: (0,) * n)


def call(
    kernel,
    name,
    scalars,
    operands,
    in_specs,
    shapes,
    out_specs=None,
    grid=(1,),
    flops=0,
    nbytes=1 << 20,
    after=(),
):
    outs = [jax.ShapeDtypeStruct(s, d) for s, d in shapes]
    first, count = 1 + len(operands), len(after)

    def body(*refs):
        kernel(*refs[:first], *refs[first + count :])

    resident = pl.BlockSpec(memory_space=pltpu.VMEM)
    place_whole = (lambda a: resident) if grid == (1,) else whole
    specs = [place_whole(a) if s is None else s for a, s in zip(operands, in_specs)]
    return pl.pallas_call(
        body,
        grid_spec=pltpu.PrefetchScalarGridSpec(
            num_scalar_prefetch=1,
            grid=grid,
            in_specs=specs + [pl.BlockSpec(memory_space=pl.ANY)] * count,
            out_specs=out_specs or [place_whole(o) for o in outs],
        ),
        out_shape=outs,
        compiler_params=PARAMS,
        cost_estimate=pl.CostEstimate(flops=flops, bytes_accessed=nbytes, transcendentals=0),
        name=name,
    )(scalars, *operands, *after)


def column(place, own, step):
    hi = place[2] if own else 1 - place[2]
    return pl.ds(pl.multiple_of((hi * NY + lax.rem(place[3] + step, NY)) * BLK, BLK), BLK)


def stage_kernel(place, student, distant, rows, *refs):
    teacher, (keep, send) = refs[:NZ], refs[NZ:]
    cross = place[1] == 0
    for k in range(NZ):
        if k < NY:
            a = student[:, column(place, True, k)]
        else:
            start = lax.rem(place[3] + k, NY) * BLK
            a = distant[:, pl.ds(pl.multiple_of(start, BLK), BLK)]
        b = teacher[k][...]
        keep[k] = jnp.where(cross, b, a)
        send[k] = jnp.where(cross, a, b)
    for k in range(2):
        send[NZ + k] = rows[:, k * BLK : k * BLK + BLK]


def stage(place, student, distant, rows, teacher):
    operands = [student, distant, rows, *teacher]
    return call(
        stage_kernel,
        "stage",
        place,
        operands,
        [None] * len(operands),
        [((n, student.shape[0], BLK), BF) for n in (NZ, NZ + 2)],
        nbytes=8 << 20,
    )


def far_half_kernel(place, student, far_half):
    width = far_half.shape[1]
    lanes = pl.ds(pl.multiple_of((1 - place[2]) * width, width), width)
    far_half[...] = student[:, lanes]


def rows_kernel(place, student, rows, slab):
    slab[...] = student[:, column(place, True, 0)]
    for k in range(2):
        wide = student[:, column(place, k == 0, 0)].astype(F32).T
        rows[k * BLK : k * BLK + BLK] = wide.astype(BF)


def sums_kernel(place, keep, send, student, keep_total, send_total):
    for target, blocks in ((keep_total, keep), (send_total, send)):
        for k in range(10):
            lanes = slice(k * BLK, k * BLK + BLK)
            if k >= NZ and target is send_total:
                target[:, lanes] = keep_total[:, lanes]
                continue
            if k < NZ:
                values = blocks[k].astype(F32)
            else:
                values = student[:, column(place, k == NZ, 0)].astype(F32)
            target[0:1, lanes] = jnp.sum(values, 0, keepdims=True)
            target[1:2, lanes] = jnp.sum(values * values, 0, keepdims=True)


def column_sums(place, keep, send, student):
    operands = [keep, send, student]
    return call(
        sums_kernel,
        "column_sums",
        place,
        operands,
        [None] * 3,
        [((2, 10 * BLK), F32)] * 2,
        nbytes=6 << 20,
    )


def tall(row, lanes):
    return jnp.broadcast_to(jnp.broadcast_to(row, (8, row.shape[1])).T[:, :1], lanes)


def pack_kernel(clips, place, own, other, out, totals, means):
    total = own[...] + other[...]
    totals[...] = total
    means[...] = tall(total[:1, 8 * BLK :] * (1.0 / clips), means.shape)
    lines = [
        total[kind : kind + 1, n * HALF : n * HALF + HALF] for kind in range(2) for n in range(20)
    ]
    rest = jnp.concatenate(lines, 0)
    terms = []
    for _ in range(3):
        term = rest.astype(BF).astype(F32)
        terms.append(term)
        rest = rest - term
    terms.append(jnp.zeros((8, HALF), F32))
    lines = jnp.concatenate(terms, 0).astype(BF)
    out[...] = jnp.concatenate([lines[:PACK], lines[PACK:]], 1)


def unpack_kernel(place, *refs):
    packed, (sums, squares) = refs[:NZ], refs[NZ:]
    square_lines = 0.0
    for k in range(NZ):
        wide = packed[k][packed[k].shape[0] - PACK :].astype(F32)
        wide = jnp.concatenate([wide[:, :HALF], wide[:, HALF:]], 0)
        lines = wide[:40] + wide[40:80] + wide[80:120]
        for n in range(20):
            sums[k : k + 1, n * HALF : n * HALF + HALF] = lines[n : n + 1]
        square_lines = square_lines + lines[20:]
    for n in range(20):
        squares[:, n * HALF : n * HALF + HALF] = square_lines[n : n + 1]


def figures_of(sums, squares, clip_total):
    center = jnp.sum(sums, 0, keepdims=True) / clip_total
    scale = lax.rsqrt(squares / clip_total - center * center + EPSILON)
    return center, scale


def half_kernel(place, rows, own, out):
    for k in range(NZ):
        out[k] = dot(rows[...], own[k], ((1,), (0,)))


def centered(means, totals, halves, other, index):
    part = halves[index]
    for k in range(2):
        part = part + dot(other[NZ + k], other[index, k * BLK : k * BLK + BLK], ((1,), (0,)))
    lanes = pl.ds(pl.multiple_of(index * BLK, BLK), BLK)
    return part - means[...] * totals[0:1, lanes]


def far_kernel(place, means, totals, halves, other, packed, top, bottom):
    index = lax.rem(place[0] + 4, NZ)
    value = centered(means, totals, halves, other, index).astype(BF)
    top[:BLK] = value[:BLK]
    bottom[:BLK] = value[BLK:]
    top[BLK:] = packed[...]
    bottom[BLK:] = packed[...]


def product_kernel(offsets, place, means, totals, halves, other, *outs):
    for k, out in zip(offsets, outs):
        index = lax.rem(place[0] + (k + NZ), NZ)
        out[...] = centered(means, totals, halves, other, index)


def gradient_kernel(
    clip_total, place, own, sums, squares, from_left, from_right, top, bottom
):
    z, core = place[0], place[1]
    clips = clip_total // NZ

    def figures(lanes):
        center, scale = figures_of(sums[:, lanes], squares[:, lanes], clip_total)
        return sums[:, lanes] * (1.0 / clips) - center, scale

    row_away, row_scale = figures(slice(8 * BLK, 10 * BLK))
    away, column_scale = figures(pl.ds(pl.multiple_of(z * BLK, BLK), BLK))
    height = 2 * BLK
    value = own[...] + from_left[:height].astype(F32) + from_right[:height].astype(F32)
    row_away = row_away.T
    for k in range(NZ):
        value = value + row_away[:, k : k + 1] * (away[k : k + 1] * float(clips))
    value = value * tall(row_scale, (height, BLK)) * (column_scale * (1.0 / clip_total))
    upper = value[:BLK]
    row = lax.broadcasted_iota(jnp.int32, (BLK, BLK), 0)
    col = lax.broadcasted_iota(jnp.int32, (BLK, BLK), 1)
    diagonal = row == col + z * BLK
    on = jnp.where(core == 0, 2.0 * (upper - 1.0), 0.0)
    upper = jnp.where(diagonal, on, upper)
    top[...] = (upper * column_scale).astype(BF)
    bottom[...] = (value[BLK:] * column_scale).astype(BF)


def reduce_rows(place, rows, means, totals, blocks, packed):
    height = 2 * BLK
    flops = 2 * rows.shape[0] * rows.shape[1] * BLK
    (halves,) = call(
        half_kernel,
        "half_products",
        place,
        [rows, blocks[0]],
        [None] * 2,
        [((NZ, rows.shape[0], BLK), F32)],
        flops=NZ * flops,
        nbytes=6 << 20,
    )

    def products(kernel, extra, count, shapes):
        operands = [means, totals, halves, blocks[1], *extra]
        return call(
            kernel,
            "products",
            place,
            operands,
            [None] * len(operands),
            shapes,
            flops=count * flops,
            nbytes=(2 + count) << 20,
        )

    def wide(*offsets):
        kernel = functools.partial(product_kernel, offsets)
        return products(kernel, (), len(offsets), [((height, BLK), F32)] * len(offsets))

    top, bottom = products(far_kernel, [packed], 1, [((BLK + PACK, BLK), BF)] * 2)
    from_left, from_right = z_shift(top, 1), z_shift(bottom, -1)
    gathered = [from_left, from_right]
    ahead, behind = wide(3, -3)
    own, *ready = wide(0, 2, -2, 1, -1)

    def add(part, arrived):
        return (part + arrived.astype(F32)).astype(BF)

    right = [add(ahead[:BLK], from_left[:BLK]), ahead[BLK:].astype(BF), from_left[BLK:]]
    left = [behind[:BLK].astype(BF), add(behind[BLK:], from_right[:BLK]), from_right[BLK:]]
    for hop in range(3):
        from_left = z_shift(jnp.concatenate(right, 0), 1)
        from_right = z_shift(jnp.concatenate(left, 0), -1)
        gathered += [from_left, from_right]
        if hop < 2:
            ahead, behind = ready[2 * hop : 2 * hop + 2]
            right = [add(ahead, from_left[:height]), from_left[height:]]
            left = [add(behind, from_right[:height]), from_right[height:]]
    return own, from_left, from_right, gathered[:-1]


def gradient(place, own, sums, squares, from_left, from_right, clip_total):
    operands = [own, sums, squares, from_left, from_right]
    return call(
        functools.partial(gradient_kernel, clip_total),
        "gradient",
        place,
        operands,
        [None] * 5,
        [((BLK, BLK), BF)] * 2,
    )


def direct_kernel(offsets, halves, has_acc, last, clip_total, place, *refs):
    count = len(offsets)
    blocks, refs = refs[:2], refs[2:]
    grads = []
    for _ in halves:
        grads.append(refs[:count])
        refs = refs[count:]
    all_sums, all_squares, refs = refs[0], refs[1], refs[2:]
    acc, square_acc, outs = (refs[0], refs[1], refs[2:]) if has_acc else (None, None, refs)
    middle = blocks[0].shape[1]
    clips = 2 * middle
    z, core = place[0], place[1]
    row = lax.broadcasted_iota(jnp.int32, (BLK, BLK), 0)
    col = lax.broadcasted_iota(jnp.int32, (BLK, BLK), 1)
    line = lax.broadcasted_iota(jnp.int32, (PAD, BLK), 0)
    lanes_of = lambda half: slice(half * BLK, half * BLK + BLK)
    total = {h: acc[:, lanes_of(h)] if has_acc else 0.0 for h in halves}
    squares = {h: square_acc[:, lanes_of(h)] if has_acc else 0.0 for h in halves}
    for k in range(count):
        index = lax.rem(z + (offsets[k] + NZ), NZ)
        lanes = pl.ds(pl.multiple_of(index * BLK, BLK), BLK)
        center, scale = figures_of(all_sums[:, lanes], all_squares[:, lanes], clip_total)
        unscale = 1.0 / scale
        means = jnp.zeros((PAD, BLK), F32)
        for n in range(3):
            high = center.astype(BF).astype(F32)
            means = jnp.where(line == n, high, means)
            center = center - high
        block = jnp.concatenate([blocks[0][index], blocks[1][index], means.astype(BF)], 0)
        for half, group in zip(halves, grads):
            grad = group[k][...]
            total[half] = total[half] + dot(block, grad, ((1,), (1,)))
            wide = grad.astype(F32) * unscale
            square = wide * wide
            if half == 0:
                diagonal = row == col + (index + core) * BLK
                square = jnp.where(diagonal, wide * (wide * 0.5 + 1.0), square)
            squares[half] = squares[half] + square
    for n, half in enumerate(halves):
        if not last:
            outs[0][:, lanes_of(half)] = total[half]
            outs[1][:, lanes_of(half)] = squares[half]
            continue
        ones = jnp.ones((PAD, BLK), BF)
        high = squares[half].astype(BF)
        low = (squares[half] - high.astype(F32)).astype(BF)
        product = dot(ones, high, ((1,), (1,))) + dot(ones, low, ((1,), (1,)))
        mean = jnp.sum(total[half][clips : clips + 3], 0, keepdims=True)
        for part in range(2):
            outs[2 * n + part][:middle] = total[half][part * middle : part * middle + middle] - mean
            outs[2 * n + part][middle:] = product


def direct_part(place, blocks, sums, squares, offsets, grads, acc, last, clip_total):
    clips = 2 * blocks[0].shape[1]
    gathered = [grads[half][k] for half in grads for k in offsets]
    operands = [*blocks, *gathered, sums, squares, *(acc or [])]
    if last:
        shapes = [((clips // 2 + PAD, BLK), F32)] * 4
    else:
        shapes = [((clips + PAD, 2 * BLK), F32), ((BLK, 2 * BLK), F32)]
    halves = tuple(grads)
    return call(
        functools.partial(direct_kernel, offsets, halves, acc is not None, last, clip_total),
        "direct_part",
        place,
        operands,
        [None] * len(operands),
        shapes,
        flops=len(halves) * len(offsets) * 2 * clips * BLK * BLK,
        nbytes=2 << 20,
    )


def body(student, teacher):
    clips = student.shape[0]
    clip_total = clips * NZ * NC
    batch = lax.axis_index("batch")
    z, core = batch // NC, batch % NC
    fj = lax.axis_index("fj")
    x_hi, y = fj // NY, fj % NY
    place = jnp.stack([z, core, x_hi, y]).astype(jnp.int32)

    def join(mine, others):
        return jnp.concatenate([mine, others], 0)

    with jax.named_scope("operand_blocks"):

        def turn(value, k):
            return move(value, lambda z, c, x, y: (z, c, x, y - k))

        def partner(value):
            return move(value, lambda z, c, x, y: (z, c, x ^ 1, y))

        around = [teacher] + [turn(teacher, k) for k in (1, 2, 3)]
        across = partner(teacher)
        (far_half,) = call(
            far_half_kernel,
            "far_half",
            place,
            [student],
            [None],
            [((clips, NY * BLK), BF)],
        )
        distant = move(far_half, lambda z, c, x, y: (z, c, far(x), y))
        across = [across, turn(across, 1), partner(around[2]), turn(across, 3)]
        teacher_blocks = around + across

    with jax.named_scope("rows"):
        rows, slab = call(
            rows_kernel,
            "rows",
            place,
            [student],
            [None],
            [((2 * BLK, clips), BF), ((clips, BLK), BF)],
        )

    with jax.named_scope("stage"):
        keep, send = stage(place, student, distant, rows, teacher_blocks)
        blocks = keep, core_swap(send)

    with jax.named_scope("statistics"):
        own_sums, other_sums = column_sums(place, keep, send, student)
        packed, totals, means = call(
            functools.partial(pack_kernel, 2 * clips),
            "pack",
            place,
            [own_sums, core_swap(other_sums)],
            [None] * 2,
            [((PACK, BLK), BF), ((2, 10 * BLK), F32), ((2 * BLK, BLK), F32)],
        )

    with jax.named_scope("reduce"):
        own, right, left, gathered = reduce_rows(
            place, rows, means, totals, blocks, packed
        )

    with jax.named_scope("statistics"):
        sums, squares = call(
            unpack_kernel,
            "unpack",
            place,
            [packed, *gathered],
            [None] * NZ,
            [((NZ, 10 * BLK), F32), ((1, 10 * BLK), F32)],
        )

    with jax.named_scope("gradient"):
        top, bottom = gradient(place, own, sums, squares, right, left, clip_total)

    with jax.named_scope("spread"):
        tops, bottoms = {0: top}, {0: bottom}
        for k in range(1, 5):
            tops[-k] = z_shift(tops[1 - k], 1)
            bottoms[k] = z_shift(bottoms[k - 1], -1)
            if k < 4:
                bottoms[-k] = z_shift(bottoms[1 - k], 1)
                tops[k] = z_shift(tops[k - 1], -1)
        tops[4] = tops[-4]

    with jax.named_scope("direct"):
        part = lambda offsets, grads, acc, last: direct_part(
            place, blocks, sums, squares, offsets, grads, acc, last, clip_total
        )
        acc = part((0, -1, 1), {0: tops, 1: bottoms}, None, False)
        acc = part((-2, 2, -3, 3), {0: tops, 1: bottoms}, acc, False)
        own_1, away_1, own_0, away_0 = part((4,), {1: bottoms, 0: tops}, acc, True)
        sent = own_1 + core_swap(away_1)
        wide = own_0 + core_swap(away_0)
        high = sent.astype(BF)
        low = (sent[clips:] - high[clips:].astype(F32)).astype(BF)
        arrived = move(join(high, low), lambda z, c, x, y: (z, c, (x + 2) % NX, y)).astype(F32)
        direct = wide[:clips] + arrived[:clips]
        product = wide[clips] + arrived[clips] + arrived[clips + PAD]

    with jax.named_scope("student_grad"):
        lanes = slice(8 * BLK, 9 * BLK)
        center, scale = figures_of(sums[:, lanes], squares[:, lanes], clip_total)
        scaled = (slab.astype(F32) - center) * scale
        return scale * (direct - scaled * product)


def solution(mesh):
    placed = (P("batch", "fi"), P("batch", ("fi", "fj")))
    return jax.shard_map(
        body, mesh=mesh, in_specs=placed, out_specs=P("batch", ("fi", "fj")), check_vma=False
    )
```

```python
import functools

import jax
import jax.numpy as jnp
from jax import lax
from jax.experimental import pallas as pl
from jax.experimental.pallas import tpu as pltpu
from jax.sharding import PartitionSpec as P

EPSILON = 1e-05
BF = jnp.bfloat16
F32 = jnp.float32
NZ, NC, NX, NY = 8, 2, 4, 4
BLK = 256
HALF = 128
PACK = 64
PAD = 16
PARAMS = pltpu.CompilerParams(vmem_limit_bytes=28 * 1024 * 1024)


def move(value, target):
    flat = lambda z, c, x, y: (z % NZ * NC + c) * 16 + x % 2 * 8 + x // 2 * NY + y % NY
    pairs = []
    for z in range(NZ):
        for c in range(NC):
            for x in range(NX):
                for y in range(NY):
                    to = target(z, c, x, y)
                    if to is not None:
                        pairs.append((flat(z, c, x, y), flat(*to)))
    return lax.ppermute(value, ("batch", "fi", "fj"), pairs)


def z_shift(value, step):
    return move(value, lambda z, c, x, y: (z + step, c, x, y))


def z_swap(value, bit):
    return move(value, lambda z, c, x, y: (z ^ bit, c, x, y))


def core_swap(value):
    return move(value, lambda z, c, x, y: (z, 1 - c, x, y))


def far(x):
    return (x + 3) % NX if x % 2 == 0 else (x + 1) % NX


def dot(a, b, dims):
    return lax.dot_general(a, b, (dims, ((), ())), preferred_element_type=F32)


def whole(a):
    return pl.BlockSpec(a.shape, lambda i, *p, n=a.ndim: (0,) * n)


def call(
    kernel,
    name,
    scalars,
    operands,
    in_specs,
    shapes,
    out_specs=None,
    grid=(1,),
    flops=0,
    nbytes=1 << 20,
    after=(),
):
    outs = [jax.ShapeDtypeStruct(s, d) for s, d in shapes]
    first, count = 1 + len(operands), len(after)

    def body(*refs):
        kernel(*refs[:first], *refs[first + count :])

    resident = pl.BlockSpec(memory_space=pltpu.VMEM)
    place_whole = (lambda a: resident) if grid == (1,) else whole
    specs = [place_whole(a) if s is None else s for a, s in zip(operands, in_specs)]
    return pl.pallas_call(
        body,
        grid_spec=pltpu.PrefetchScalarGridSpec(
            num_scalar_prefetch=1,
            grid=grid,
            in_specs=specs + [pl.BlockSpec(memory_space=pl.ANY)] * count,
            out_specs=out_specs or [place_whole(o) for o in outs],
        ),
        out_shape=outs,
        compiler_params=PARAMS,
        cost_estimate=pl.CostEstimate(flops=flops, bytes_accessed=nbytes, transcendentals=0),
        name=name,
    )(scalars, *operands, *after)


def column(place, own, step):
    hi = place[2] if own else 1 - place[2]
    return pl.ds(pl.multiple_of((hi * NY + lax.rem(place[3] + step, NY)) * BLK, BLK), BLK)


def stage_kernel(place, student, distant, rows, *refs):
    teacher, (keep, send) = refs[:NZ], refs[NZ:]
    cross = place[1] == 0
    for k in range(NZ):
        if k < NY:
            a = student[:, column(place, True, k)]
        else:
            start = lax.rem(place[3] + k, NY) * BLK
            a = distant[:, pl.ds(pl.multiple_of(start, BLK), BLK)]
        b = teacher[k][...]
        keep[k] = jnp.where(cross, b, a)
        send[k] = jnp.where(cross, a, b)
    for k in range(2):
        send[NZ + k] = rows[:, k * BLK : k * BLK + BLK]


def stage(place, student, distant, rows, teacher):
    operands = [student, distant, rows, *teacher]
    return call(
        stage_kernel,
        "stage",
        place,
        operands,
        [None] * len(operands),
        [((n, student.shape[0], BLK), BF) for n in (NZ, NZ + 2)],
        nbytes=8 << 20,
    )


def far_half_kernel(place, student, far_half):
    width = far_half.shape[1]
    lanes = pl.ds(pl.multiple_of((1 - place[2]) * width, width), width)
    far_half[...] = student[:, lanes]


def rows_kernel(place, student, rows, slab):
    slab[...] = student[:, column(place, True, 0)]
    for k in range(2):
        wide = student[:, column(place, k == 0, 0)].astype(F32).T
        rows[k * BLK : k * BLK + BLK] = wide.astype(BF)


def sums_kernel(place, keep, send, student, keep_total, send_total):
    for target, blocks in ((keep_total, keep), (send_total, send)):
        for k in range(10):
            lanes = slice(k * BLK, k * BLK + BLK)
            if k >= NZ and target is send_total:
                target[:, lanes] = keep_total[:, lanes]
                continue
            if k < NZ:
                values = blocks[k].astype(F32)
            else:
                values = student[:, column(place, k == NZ, 0)].astype(F32)
            target[0:1, lanes] = jnp.sum(values, 0, keepdims=True)
            target[1:2, lanes] = jnp.sum(values * values, 0, keepdims=True)


def column_sums(place, keep, send, student):
    operands = [keep, send, student]
    return call(
        sums_kernel,
        "column_sums",
        place,
        operands,
        [None] * 3,
        [((2, 10 * BLK), F32)] * 2,
        nbytes=6 << 20,
    )


def tall(row, lanes):
    return jnp.broadcast_to(jnp.broadcast_to(row, (8, row.shape[1])).T[:, :1], lanes)


def pack_kernel(clips, place, own, other, out, totals, means):
    total = own[...] + other[...]
    totals[...] = total
    means[...] = tall(total[:1, 8 * BLK :] * (1.0 / clips), means.shape)
    lines = [
        total[kind : kind + 1, n * HALF : n * HALF + HALF] for kind in range(2) for n in range(20)
    ]
    rest = jnp.concatenate(lines, 0)
    terms = []
    for _ in range(3):
        term = rest.astype(BF).astype(F32)
        terms.append(term)
        rest = rest - term
    terms.append(jnp.zeros((8, HALF), F32))
    lines = jnp.concatenate(terms, 0).astype(BF)
    out[...] = jnp.concatenate([lines[:PACK], lines[PACK:]], 1)


def unpack_kernel(place, *refs):
    packed, (sums, squares) = refs[:NZ], refs[NZ:]
    square_lines = 0.0
    for k in range(NZ):
        wide = packed[k][packed[k].shape[0] - PACK :].astype(F32)
        wide = jnp.concatenate([wide[:, :HALF], wide[:, HALF:]], 0)
        lines = wide[:40] + wide[40:80] + wide[80:120]
        for n in range(20):
            sums[k : k + 1, n * HALF : n * HALF + HALF] = lines[n : n + 1]
        square_lines = square_lines + lines[20:]
    for n in range(20):
        squares[:, n * HALF : n * HALF + HALF] = square_lines[n : n + 1]


def figures_of(sums, squares, clip_total):
    center = jnp.sum(sums, 0, keepdims=True) / clip_total
    scale = lax.rsqrt(squares / clip_total - center * center + EPSILON)
    return center, scale


def half_kernel(place, rows, own, out):
    for k in range(NZ):
        out[k] = dot(rows[...], own[k], ((1,), (0,)))


def centered(means, totals, halves, other, index):
    part = halves[index]
    for k in range(2):
        part = part + dot(other[NZ + k], other[index, k * BLK : k * BLK + BLK], ((1,), (0,)))
    lanes = pl.ds(pl.multiple_of(index * BLK, BLK), BLK)
    return part - means[...] * totals[0:1, lanes]


def far_kernel(place, means, totals, halves, other, packed, top, bottom):
    index = lax.rem(place[0] + 4, NZ)
    value = centered(means, totals, halves, other, index).astype(BF)
    top[:BLK] = value[:BLK]
    bottom[:BLK] = value[BLK:]
    top[BLK:] = packed[...]
    bottom[BLK:] = packed[...]


def product_kernel(offsets, place, means, totals, halves, other, *outs):
    for k, out in zip(offsets, outs):
        index = lax.rem(place[0] + (k + NZ), NZ)
        out[...] = centered(means, totals, halves, other, index)


def gradient_kernel(
    clip_total, place, own, from_left, from_right, *refs
):
    z, core = place[0], place[1]
    clips = clip_total // NZ
    packed, (top, bottom, sums, squares) = refs[:NZ], refs[NZ:]
    unpack_kernel(place, *packed, sums, squares)

    def figures(lanes):
        center, scale = figures_of(sums[:, lanes], squares[:, lanes], clip_total)
        return sums[:, lanes] * (1.0 / clips) - center, scale

    row_away, row_scale = figures(slice(8 * BLK, 10 * BLK))
    away, column_scale = figures(pl.ds(pl.multiple_of(z * BLK, BLK), BLK))
    height = 2 * BLK
    value = own[...] + from_left[:height].astype(F32) + from_right[:height].astype(F32)
    row_away = row_away.T
    for k in range(NZ):
        value = value + row_away[:, k : k + 1] * (away[k : k + 1] * float(clips))
    value = value * tall(row_scale, (height, BLK)) * (column_scale * (1.0 / clip_total))
    upper = value[:BLK]
    row = lax.broadcasted_iota(jnp.int32, (BLK, BLK), 0)
    col = lax.broadcasted_iota(jnp.int32, (BLK, BLK), 1)
    diagonal = row == col + z * BLK
    on = jnp.where(core == 0, 2.0 * (upper - 1.0), 0.0)
    upper = jnp.where(diagonal, on, upper)
    top[...] = (upper * column_scale).astype(BF)
    bottom[...] = (value[BLK:] * column_scale).astype(BF)


def reduce_rows(place, rows, means, totals, blocks, packed):
    height = 2 * BLK
    flops = 2 * rows.shape[0] * rows.shape[1] * BLK
    (halves,) = call(
        half_kernel,
        "half_products",
        place,
        [rows, blocks[0]],
        [None] * 2,
        [((NZ, rows.shape[0], BLK), F32)],
        flops=NZ * flops,
        nbytes=6 << 20,
    )

    def products(kernel, extra, count, shapes):
        operands = [means, totals, halves, blocks[1], *extra]
        return call(
            kernel,
            "products",
            place,
            operands,
            [None] * len(operands),
            shapes,
            flops=count * flops,
            nbytes=(2 + count) << 20,
        )

    def wide(*offsets):
        kernel = functools.partial(product_kernel, offsets)
        return products(kernel, (), len(offsets), [((height, BLK), F32)] * len(offsets))

    top, bottom = products(far_kernel, [packed], 1, [((BLK + PACK, BLK), BF)] * 2)
    from_left, from_right = z_shift(top, 1), z_shift(bottom, -1)
    gathered = [from_left, from_right]
    ahead, behind = wide(3, -3)
    own, *ready = wide(0, 2, -2, 1, -1)

    def add(part, arrived):
        return (part + arrived.astype(F32)).astype(BF)

    right = [add(ahead[:BLK], from_left[:BLK]), ahead[BLK:].astype(BF), from_left[BLK:]]
    left = [behind[:BLK].astype(BF), add(behind[BLK:], from_right[:BLK]), from_right[BLK:]]
    for hop in range(3):
        from_left = z_shift(jnp.concatenate(right, 0), 1)
        from_right = z_shift(jnp.concatenate(left, 0), -1)
        gathered += [from_left, from_right]
        if hop < 2:
            ahead, behind = ready[2 * hop : 2 * hop + 2]
            right = [add(ahead, from_left[:height]), from_left[height:]]
            left = [add(behind, from_right[:height]), from_right[height:]]
            if hop == 1:
                left = left[:1]
    return own, from_left, from_right, gathered[:-1]


def gradient(place, own, from_left, from_right, packed, clip_total):
    operands = [own, from_left, from_right, *packed]
    return call(
        functools.partial(gradient_kernel, clip_total),
        "gradient",
        place,
        operands,
        [None] * len(operands),
        [((BLK, BLK), BF)] * 2 + [((NZ, 10 * BLK), F32), ((1, 10 * BLK), F32)],
    )


def direct_kernel(offsets, halves, has_acc, last, clip_total, place, *refs):
    count = len(offsets)
    blocks, refs = refs[:2], refs[2:]
    grads = []
    for _ in halves:
        grads.append(refs[:count])
        refs = refs[count:]
    all_sums, all_squares, refs = refs[0], refs[1], refs[2:]
    acc, square_acc, outs = (refs[0], refs[1], refs[2:]) if has_acc else (None, None, refs)
    middle = blocks[0].shape[1]
    clips = 2 * middle
    z, core = place[0], place[1]
    row = lax.broadcasted_iota(jnp.int32, (BLK, BLK), 0)
    col = lax.broadcasted_iota(jnp.int32, (BLK, BLK), 1)
    line = lax.broadcasted_iota(jnp.int32, (PAD, BLK), 0)
    lanes_of = lambda half: slice(half * BLK, half * BLK + BLK)
    total = {h: acc[:, lanes_of(h)] if has_acc else 0.0 for h in halves}
    squares = {h: square_acc[:, lanes_of(h)] if has_acc else 0.0 for h in halves}
    for k in range(count):
        index = lax.rem(z + (offsets[k] + NZ), NZ)
        lanes = pl.ds(pl.multiple_of(index * BLK, BLK), BLK)
        center, scale = figures_of(all_sums[:, lanes], all_squares[:, lanes], clip_total)
        unscale = 1.0 / scale
        means = jnp.zeros((PAD, BLK), F32)
        for n in range(3):
            high = center.astype(BF).astype(F32)
            means = jnp.where(line == n, high, means)
            center = center - high
        block = jnp.concatenate([blocks[0][index], blocks[1][index], means.astype(BF)], 0)
        for half, group in zip(halves, grads):
            grad = group[k][...]
            total[half] = total[half] + dot(block, grad, ((1,), (1,)))
            wide = grad.astype(F32) * unscale
            square = wide * wide
            if half == 0:
                diagonal = row == col + (index + core) * BLK
                square = jnp.where(diagonal, wide * (wide * 0.5 + 1.0), square)
            squares[half] = squares[half] + square
    for n, half in enumerate(halves):
        if not last:
            outs[0][:, lanes_of(half)] = total[half]
            outs[1][:, lanes_of(half)] = squares[half]
            continue
        ones = jnp.ones((PAD, BLK), BF)
        high = squares[half].astype(BF)
        low = (squares[half] - high.astype(F32)).astype(BF)
        product = dot(ones, high, ((1,), (1,))) + dot(ones, low, ((1,), (1,)))
        mean = jnp.sum(total[half][clips : clips + 3], 0, keepdims=True)
        for part in range(2):
            outs[2 * n + part][:middle] = total[half][part * middle : part * middle + middle] - mean
            outs[2 * n + part][middle:] = product


def direct_part(place, blocks, sums, squares, offsets, grads, acc, last, clip_total):
    clips = 2 * blocks[0].shape[1]
    gathered = [grads[half][k] for half in grads for k in offsets]
    operands = [*blocks, *gathered, sums, squares, *(acc or [])]
    if last:
        shapes = [((clips // 2 + PAD, BLK), F32)] * 4
    else:
        shapes = [((clips + PAD, 2 * BLK), F32), ((BLK, 2 * BLK), F32)]
    halves = tuple(grads)
    return call(
        functools.partial(direct_kernel, offsets, halves, acc is not None, last, clip_total),
        "direct_part",
        place,
        operands,
        [None] * len(operands),
        shapes,
        flops=len(halves) * len(offsets) * 2 * clips * BLK * BLK,
        nbytes=2 << 20,
    )


def body(student, teacher):
    clips = student.shape[0]
    clip_total = clips * NZ * NC
    batch = lax.axis_index("batch")
    z, core = batch // NC, batch % NC
    fj = lax.axis_index("fj")
    x_hi, y = fj // NY, fj % NY
    place = jnp.stack([z, core, x_hi, y]).astype(jnp.int32)

    def join(mine, others):
        return jnp.concatenate([mine, others], 0)

    with jax.named_scope("operand_blocks"):

        def turn(value, k):
            return move(value, lambda z, c, x, y: (z, c, x, y - k))

        def partner(value):
            return move(value, lambda z, c, x, y: (z, c, x ^ 1, y))

        around = [teacher] + [turn(teacher, k) for k in (1, 2, 3)]
        across = partner(teacher)
        (far_half,) = call(
            far_half_kernel,
            "far_half",
            place,
            [student],
            [None],
            [((clips, NY * BLK), BF)],
        )
        distant = move(far_half, lambda z, c, x, y: (z, c, far(x), y))
        across = [across, turn(across, 1), partner(around[2]), turn(across, 3)]
        teacher_blocks = around + across

    with jax.named_scope("rows"):
        rows, slab = call(
            rows_kernel,
            "rows",
            place,
            [student],
            [None],
            [((2 * BLK, clips), BF), ((clips, BLK), BF)],
        )

    with jax.named_scope("stage"):
        keep, send = stage(place, student, distant, rows, teacher_blocks)
        blocks = keep, core_swap(send)

    with jax.named_scope("statistics"):
        own_sums, other_sums = column_sums(place, keep, send, student)
        packed, totals, means = call(
            functools.partial(pack_kernel, 2 * clips),
            "pack",
            place,
            [own_sums, core_swap(other_sums)],
            [None] * 2,
            [((PACK, BLK), BF), ((2, 10 * BLK), F32), ((2 * BLK, BLK), F32)],
        )

    with jax.named_scope("reduce"):
        own, right, left, gathered = reduce_rows(
            place, rows, means, totals, blocks, packed
        )

    with jax.named_scope("gradient"):
        top, bottom, sums, squares = gradient(
            place, own, right, left, [packed, *gathered], clip_total
        )

    with jax.named_scope("spread"):
        tops, bottoms = {0: top}, {0: bottom}
        for k in range(1, 5):
            tops[-k] = z_shift(tops[1 - k], 1)
            bottoms[k] = z_shift(bottoms[k - 1], -1)
            if k < 4:
                bottoms[-k] = z_shift(bottoms[1 - k], 1)
                tops[k] = z_shift(tops[k - 1], -1)
        tops[4] = tops[-4]

    with jax.named_scope("direct"):
        part = lambda offsets, grads, acc, last: direct_part(
            place, blocks, sums, squares, offsets, grads, acc, last, clip_total
        )
        acc = part((0, -1, 1), {0: tops, 1: bottoms}, None, False)
        acc = part((-2, 2, -3, 3), {0: tops, 1: bottoms}, acc, False)
        own_1, away_1, own_0, away_0 = part((4,), {1: bottoms, 0: tops}, acc, True)
        sent = own_1 + core_swap(away_1)
        wide = own_0 + core_swap(away_0)
        high = sent.astype(BF)
        low = (sent[clips:] - high[clips:].astype(F32)).astype(BF)
        arrived = move(join(high, low), lambda z, c, x, y: (z, c, (x + 2) % NX, y)).astype(F32)
        direct = wide[:clips] + arrived[:clips]
        product = wide[clips] + arrived[clips] + arrived[clips + PAD]

    with jax.named_scope("student_grad"):
        lanes = slice(8 * BLK, 9 * BLK)
        center, scale = figures_of(sums[:, lanes], squares[:, lanes], clip_total)
        scaled = (slab.astype(F32) - center) * scale
        return scale * (direct - scaled * product)


def solution(mesh):
    placed = (P("batch", "fi"), P("batch", ("fi", "fj")))
    return jax.shard_map(
        body, mesh=mesh, in_specs=placed, out_specs=P("batch", ("fi", "fj")), check_vma=False
    )
```

```python
import functools

import jax
import jax.numpy as jnp
from jax import lax
from jax.experimental import pallas as pl
from jax.experimental.pallas import tpu as pltpu
from jax.sharding import PartitionSpec as P

EPSILON = 1e-05
BF = jnp.bfloat16
F32 = jnp.float32
NZ, NC, NX, NY = 8, 2, 4, 4
BLK = 256
HALF = 128
PACK = 64
PAD = 16
PARAMS = pltpu.CompilerParams(vmem_limit_bytes=28 * 1024 * 1024)


def move(value, target):
    flat = lambda z, c, x, y: (z % NZ * NC + c) * 16 + x % 2 * 8 + x // 2 * NY + y % NY
    pairs = []
    for z in range(NZ):
        for c in range(NC):
            for x in range(NX):
                for y in range(NY):
                    to = target(z, c, x, y)
                    if to is not None:
                        pairs.append((flat(z, c, x, y), flat(*to)))
    return lax.ppermute(value, ("batch", "fi", "fj"), pairs)


def z_shift(value, step):
    return move(value, lambda z, c, x, y: (z + step, c, x, y))


def z_swap(value, bit):
    return move(value, lambda z, c, x, y: (z ^ bit, c, x, y))


def core_swap(value):
    return move(value, lambda z, c, x, y: (z, 1 - c, x, y))


def far(x):
    return (x + 3) % NX if x % 2 == 0 else (x + 1) % NX


def dot(a, b, dims):
    return lax.dot_general(a, b, (dims, ((), ())), preferred_element_type=F32)


def whole(a):
    return pl.BlockSpec(a.shape, lambda i, *p, n=a.ndim: (0,) * n)


def call(
    kernel,
    name,
    scalars,
    operands,
    in_specs,
    shapes,
    out_specs=None,
    grid=(1,),
    flops=0,
    nbytes=1 << 20,
    after=(),
):
    outs = [jax.ShapeDtypeStruct(s, d) for s, d in shapes]
    first, count = 1 + len(operands), len(after)

    def body(*refs):
        kernel(*refs[:first], *refs[first + count :])

    resident = pl.BlockSpec(memory_space=pltpu.VMEM)
    place_whole = (lambda a: resident) if grid == (1,) else whole
    specs = [place_whole(a) if s is None else s for a, s in zip(operands, in_specs)]
    return pl.pallas_call(
        body,
        grid_spec=pltpu.PrefetchScalarGridSpec(
            num_scalar_prefetch=1,
            grid=grid,
            in_specs=specs + [pl.BlockSpec(memory_space=pl.ANY)] * count,
            out_specs=out_specs or [place_whole(o) for o in outs],
        ),
        out_shape=outs,
        compiler_params=PARAMS,
        cost_estimate=pl.CostEstimate(flops=flops, bytes_accessed=nbytes, transcendentals=0),
        name=name,
    )(scalars, *operands, *after)


def column(place, own, step):
    hi = place[2] if own else 1 - place[2]
    return pl.ds(pl.multiple_of((hi * NY + lax.rem(place[3] + step, NY)) * BLK, BLK), BLK)


def stage_kernel(place, student, distant, rows, *refs):
    teacher, (keep, send) = refs[:NZ], refs[NZ:]
    cross = place[1] == 0
    for k in range(NZ):
        if k < NY:
            a = student[:, column(place, True, k)]
        else:
            start = lax.rem(place[3] + k, NY) * BLK
            a = distant[:, pl.ds(pl.multiple_of(start, BLK), BLK)]
        b = teacher[k][...]
        keep[k] = jnp.where(cross, b, a)
        send[k] = jnp.where(cross, a, b)
    for k in range(2):
        send[NZ + k] = rows[:, k * BLK : k * BLK + BLK]


def stage(place, student, distant, rows, teacher):
    operands = [student, distant, rows, *teacher]
    return call(
        stage_kernel,
        "stage",
        place,
        operands,
        [None] * len(operands),
        [((n, student.shape[0], BLK), BF) for n in (NZ, NZ + 2)],
        nbytes=8 << 20,
    )


def far_half_kernel(place, student, far_half):
    width = far_half.shape[1]
    lanes = pl.ds(pl.multiple_of((1 - place[2]) * width, width), width)
    far_half[...] = student[:, lanes]


def rows_kernel(place, student, rows, slab):
    slab[...] = student[:, column(place, True, 0)]
    for k in range(2):
        wide = student[:, column(place, k == 0, 0)].astype(F32).T
        rows[k * BLK : k * BLK + BLK] = wide.astype(BF)


def sums_kernel(place, keep, send, student, keep_total, send_total):
    for target, blocks in ((keep_total, keep), (send_total, send)):
        for k in range(10):
            lanes = slice(k * BLK, k * BLK + BLK)
            if k >= NZ and target is send_total:
                target[:, lanes] = keep_total[:, lanes]
                continue
            if k < NZ:
                values = blocks[k].astype(F32)
            else:
                values = student[:, column(place, k == NZ, 0)].astype(F32)
            target[0:1, lanes] = jnp.sum(values, 0, keepdims=True)
            target[1:2, lanes] = jnp.sum(values * values, 0, keepdims=True)


def column_sums(place, keep, send, student):
    operands = [keep, send, student]
    return call(
        sums_kernel,
        "column_sums",
        place,
        operands,
        [None] * 3,
        [((2, 10 * BLK), F32)] * 2,
        nbytes=6 << 20,
    )


def tall(row, lanes):
    return jnp.broadcast_to(jnp.broadcast_to(row, (8, row.shape[1])).T[:, :1], lanes)


def pack_kernel(clips, place, own, other, out, totals, means):
    total = own[...] + other[...]
    totals[...] = total
    means[...] = tall(total[:1, 8 * BLK :] * (1.0 / clips), means.shape)
    lines = [
        total[kind : kind + 1, n * HALF : n * HALF + HALF] for kind in range(2) for n in range(20)
    ]
    rest = jnp.concatenate(lines, 0)
    terms = []
    for _ in range(3):
        term = rest.astype(BF).astype(F32)
        terms.append(term)
        rest = rest - term
    terms.append(jnp.zeros((8, HALF), F32))
    lines = jnp.concatenate(terms, 0).astype(BF)
    out[...] = jnp.concatenate([lines[:PACK], lines[PACK:]], 1)


def unpack_kernel(place, *refs):
    packed, (sums, squares) = refs[:NZ], refs[NZ:]
    square_lines = 0.0
    for k in range(NZ):
        wide = packed[k][packed[k].shape[0] - PACK :].astype(F32)
        wide = jnp.concatenate([wide[:, :HALF], wide[:, HALF:]], 0)
        lines = wide[:40] + wide[40:80] + wide[80:120]
        for n in range(20):
            sums[k : k + 1, n * HALF : n * HALF + HALF] = lines[n : n + 1]
        square_lines = square_lines + lines[20:]
    for n in range(20):
        squares[:, n * HALF : n * HALF + HALF] = square_lines[n : n + 1]


def figures_of(sums, squares, clip_total):
    center = jnp.sum(sums, 0, keepdims=True) / clip_total
    scale = lax.rsqrt(squares / clip_total - center * center + EPSILON)
    return center, scale


def half_kernel(place, rows, own, out):
    for k in range(NZ):
        out[k] = dot(rows[...], own[k], ((1,), (0,)))


def centered(means, totals, halves, other, index):
    part = halves[index]
    for k in range(2):
        part = part + dot(other[NZ + k], other[index, k * BLK : k * BLK + BLK], ((1,), (0,)))
    lanes = pl.ds(pl.multiple_of(index * BLK, BLK), BLK)
    return part - means[...] * totals[0:1, lanes]


def far_kernel(place, own_sums, other_sums, halves, other, *outs):
    top, bottom, packed, totals, means = outs
    pack_kernel(2 * other.shape[1], place, own_sums, other_sums, packed, totals, means)
    index = lax.rem(place[0] + 4, NZ)
    value = centered(means, totals, halves, other, index).astype(BF)
    top[:BLK] = value[:BLK]
    bottom[:BLK] = value[BLK:]
    top[BLK:] = packed[...]
    bottom[BLK:] = packed[...]


def product_kernel(offsets, place, means, totals, halves, other, *outs):
    for k, out in zip(offsets, outs):
        index = lax.rem(place[0] + (k + NZ), NZ)
        out[...] = centered(means, totals, halves, other, index)


def gradient_kernel(
    clip_total, place, own, from_left, from_right, *refs
):
    z, core = place[0], place[1]
    clips = clip_total // NZ
    packed, (top, bottom, sums, squares) = refs[:NZ], refs[NZ:]
    unpack_kernel(place, *packed, sums, squares)

    def figures(lanes):
        center, scale = figures_of(sums[:, lanes], squares[:, lanes], clip_total)
        return sums[:, lanes] * (1.0 / clips) - center, scale

    row_away, row_scale = figures(slice(8 * BLK, 10 * BLK))
    away, column_scale = figures(pl.ds(pl.multiple_of(z * BLK, BLK), BLK))
    height = 2 * BLK
    value = own[...] + from_left[:height].astype(F32) + from_right[:height].astype(F32)
    row_away = row_away.T
    for k in range(NZ):
        value = value + row_away[:, k : k + 1] * (away[k : k + 1] * float(clips))
    value = value * tall(row_scale, (height, BLK)) * (column_scale * (1.0 / clip_total))
    upper = value[:BLK]
    row = lax.broadcasted_iota(jnp.int32, (BLK, BLK), 0)
    col = lax.broadcasted_iota(jnp.int32, (BLK, BLK), 1)
    diagonal = row == col + z * BLK
    on = jnp.where(core == 0, 2.0 * (upper - 1.0), 0.0)
    upper = jnp.where(diagonal, on, upper)
    top[...] = (upper * column_scale).astype(BF)
    bottom[...] = (value[BLK:] * column_scale).astype(BF)


def reduce_rows(place, rows, sums, blocks):
    height = 2 * BLK
    flops = 2 * rows.shape[0] * rows.shape[1] * BLK
    (halves,) = call(
        half_kernel,
        "half_products",
        place,
        [rows, blocks[0]],
        [None] * 2,
        [((NZ, rows.shape[0], BLK), F32)],
        flops=NZ * flops,
        nbytes=6 << 20,
    )

    def products(kernel, figures, count, shapes):
        operands = [*figures, halves, blocks[1]]
        return call(
            kernel,
            "products",
            place,
            operands,
            [None] * len(operands),
            shapes,
            flops=count * flops,
            nbytes=(2 + count) << 20,
        )

    def wide(*offsets):
        kernel = functools.partial(product_kernel, offsets)
        return products(kernel, (means, totals), len(offsets), [((height, BLK), F32)] * len(offsets))

    shapes = [((BLK + PACK, BLK), BF)] * 2
    shapes += [((PACK, BLK), BF), ((2, 10 * BLK), F32), ((height, BLK), F32)]
    top, bottom, packed, totals, means = products(far_kernel, sums, 1, shapes)
    from_left, from_right = z_shift(top, 1), z_shift(bottom, -1)
    gathered = [from_left, from_right]
    ahead, behind = wide(3, -3)
    own, *ready = wide(0, 2, -2, 1, -1)

    def add(part, arrived):
        return (part + arrived.astype(F32)).astype(BF)

    right = [add(ahead[:BLK], from_left[:BLK]), ahead[BLK:].astype(BF), from_left[BLK:]]
    left = [behind[:BLK].astype(BF), add(behind[BLK:], from_right[:BLK]), from_right[BLK:]]
    for hop in range(3):
        from_left = z_shift(jnp.concatenate(right, 0), 1)
        from_right = z_shift(jnp.concatenate(left, 0), -1)
        gathered += [from_left, from_right]
        if hop < 2:
            ahead, behind = ready[2 * hop : 2 * hop + 2]
            right = [add(ahead, from_left[:height]), from_left[height:]]
            left = [add(behind, from_right[:height]), from_right[height:]]
            if hop == 1:
                left = left[:1]
    return own, from_left, from_right, [packed, *gathered[:-1]]


def gradient(place, own, from_left, from_right, packed, clip_total):
    operands = [own, from_left, from_right, *packed]
    return call(
        functools.partial(gradient_kernel, clip_total),
        "gradient",
        place,
        operands,
        [None] * len(operands),
        [((BLK, BLK), BF)] * 2 + [((NZ, 10 * BLK), F32), ((1, 10 * BLK), F32)],
    )


def direct_kernel(offsets, halves, has_acc, last, clip_total, place, *refs):
    count = len(offsets)
    blocks, refs = refs[:2], refs[2:]
    grads = []
    for _ in halves:
        grads.append(refs[:count])
        refs = refs[count:]
    all_sums, all_squares, refs = refs[0], refs[1], refs[2:]
    acc, square_acc, outs = (refs[0], refs[1], refs[2:]) if has_acc else (None, None, refs)
    middle = blocks[0].shape[1]
    clips = 2 * middle
    z, core = place[0], place[1]
    row = lax.broadcasted_iota(jnp.int32, (BLK, BLK), 0)
    col = lax.broadcasted_iota(jnp.int32, (BLK, BLK), 1)
    line = lax.broadcasted_iota(jnp.int32, (PAD, BLK), 0)
    lanes_of = lambda half: slice(half * BLK, half * BLK + BLK)
    total = {h: acc[:, lanes_of(h)] if has_acc else 0.0 for h in halves}
    squares = {h: square_acc[:, lanes_of(h)] if has_acc else 0.0 for h in halves}
    for k in range(count):
        index = lax.rem(z + (offsets[k] + NZ), NZ)
        lanes = pl.ds(pl.multiple_of(index * BLK, BLK), BLK)
        center, scale = figures_of(all_sums[:, lanes], all_squares[:, lanes], clip_total)
        unscale = 1.0 / scale
        means = jnp.zeros((PAD, BLK), F32)
        for n in range(3):
            high = center.astype(BF).astype(F32)
            means = jnp.where(line == n, high, means)
            center = center - high
        block = jnp.concatenate([blocks[0][index], blocks[1][index], means.astype(BF)], 0)
        for half, group in zip(halves, grads):
            grad = group[k][...]
            total[half] = total[half] + dot(block, grad, ((1,), (1,)))
            wide = grad.astype(F32) * unscale
            square = wide * wide
            if half == 0:
                diagonal = row == col + (index + core) * BLK
                square = jnp.where(diagonal, wide * (wide * 0.5 + 1.0), square)
            squares[half] = squares[half] + square
    for n, half in enumerate(halves):
        if not last:
            outs[0][:, lanes_of(half)] = total[half]
            outs[1][:, lanes_of(half)] = squares[half]
            continue
        ones = jnp.ones((PAD, BLK), BF)
        high = squares[half].astype(BF)
        low = (squares[half] - high.astype(F32)).astype(BF)
        product = dot(ones, high, ((1,), (1,))) + dot(ones, low, ((1,), (1,)))
        mean = jnp.sum(total[half][clips : clips + 3], 0, keepdims=True)
        for part in range(2):
            outs[2 * n + part][:middle] = total[half][part * middle : part * middle + middle] - mean
            outs[2 * n + part][middle:] = product


def direct_part(place, blocks, sums, squares, offsets, grads, acc, last, clip_total):
    clips = 2 * blocks[0].shape[1]
    gathered = [grads[half][k] for half in grads for k in offsets]
    operands = [*blocks, *gathered, sums, squares, *(acc or [])]
    if last:
        shapes = [((clips // 2 + PAD, BLK), F32)] * 4
    else:
        shapes = [((clips + PAD, 2 * BLK), F32), ((BLK, 2 * BLK), F32)]
    halves = tuple(grads)
    return call(
        functools.partial(direct_kernel, offsets, halves, acc is not None, last, clip_total),
        "direct_part",
        place,
        operands,
        [None] * len(operands),
        shapes,
        flops=len(halves) * len(offsets) * 2 * clips * BLK * BLK,
        nbytes=2 << 20,
    )


def body(student, teacher):
    clips = student.shape[0]
    clip_total = clips * NZ * NC
    batch = lax.axis_index("batch")
    z, core = batch // NC, batch % NC
    fj = lax.axis_index("fj")
    x_hi, y = fj // NY, fj % NY
    place = jnp.stack([z, core, x_hi, y]).astype(jnp.int32)

    def join(mine, others):
        return jnp.concatenate([mine, others], 0)

    with jax.named_scope("operand_blocks"):

        def turn(value, k):
            return move(value, lambda z, c, x, y: (z, c, x, y - k))

        def partner(value):
            return move(value, lambda z, c, x, y: (z, c, x ^ 1, y))

        around = [teacher] + [turn(teacher, k) for k in (1, 2, 3)]
        across = partner(teacher)
        (far_half,) = call(
            far_half_kernel,
            "far_half",
            place,
            [student],
            [None],
            [((clips, NY * BLK), BF)],
        )
        distant = move(far_half, lambda z, c, x, y: (z, c, far(x), y))
        across = [across, turn(across, 1), partner(around[2]), turn(across, 3)]
        teacher_blocks = around + across

    with jax.named_scope("rows"):
        rows, slab = call(
            rows_kernel,
            "rows",
            place,
            [student],
            [None],
            [((2 * BLK, clips), BF), ((clips, BLK), BF)],
        )

    with jax.named_scope("stage"):
        keep, send = stage(place, student, distant, rows, teacher_blocks)
        blocks = keep, core_swap(send)

    with jax.named_scope("statistics"):
        own_sums, other_sums = column_sums(place, keep, send, student)
        sums = own_sums, core_swap(other_sums)

    with jax.named_scope("reduce"):
        own, right, left, gathered = reduce_rows(
            place, rows, sums, blocks
        )

    with jax.named_scope("gradient"):
        top, bottom, sums, squares = gradient(
            place, own, right, left, gathered, clip_total
        )

    with jax.named_scope("spread"):
        tops, bottoms = {0: top}, {0: bottom}
        for k in range(1, 5):
            tops[-k] = z_shift(tops[1 - k], 1)
            bottoms[k] = z_shift(bottoms[k - 1], -1)
            if k < 4:
                bottoms[-k] = z_shift(bottoms[1 - k], 1)
                tops[k] = z_shift(tops[k - 1], -1)
        tops[4] = tops[-4]

    with jax.named_scope("direct"):
        part = lambda offsets, grads, acc, last: direct_part(
            place, blocks, sums, squares, offsets, grads, acc, last, clip_total
        )
        acc = part((0, -1, 1), {0: tops, 1: bottoms}, None, False)
        acc = part((-2, 2, -3, 3), {0: tops, 1: bottoms}, acc, False)
        own_1, away_1, own_0, away_0 = part((4,), {1: bottoms, 0: tops}, acc, True)
        sent = own_1 + core_swap(away_1)
        wide = own_0 + core_swap(away_0)
        high = sent.astype(BF)
        low = (sent[clips:] - high[clips:].astype(F32)).astype(BF)
        arrived = move(join(high, low), lambda z, c, x, y: (z, c, (x + 2) % NX, y)).astype(F32)
        direct = wide[:clips] + arrived[:clips]
        product = wide[clips] + arrived[clips] + arrived[clips + PAD]

    with jax.named_scope("student_grad"):
        lanes = slice(8 * BLK, 9 * BLK)
        center, scale = figures_of(sums[:, lanes], squares[:, lanes], clip_total)
        scaled = (slab.astype(F32) - center) * scale
        return scale * (direct - scaled * product)


def solution(mesh):
    placed = (P("batch", "fi"), P("batch", ("fi", "fj")))
    return jax.shard_map(
        body, mesh=mesh, in_specs=placed, out_specs=P("batch", ("fi", "fj")), check_vma=False
    )
```
